256 devices in a mesh: seq: 128 (over z, x, y), head: 2 (over core).
Axes of the slice: x: 4, y: 4, z: 8, core: 2. Of those that a mesh axis runs over, the one named last changes fastest.
Arguments:
- queries: bfloat16 [16384, 2048], P(('seq', 'head')), may hold values from -5 to 5
- new_keys: bfloat16 [16384, 2048], P(('seq', 'head')), may hold values from -5 to 5
- new_values: bfloat16 [16384, 2048], P(('seq', 'head')), may hold values from -12 to 12
- grad_out: bfloat16 [16384, 2048], P(('seq', 'head')), may hold values from -192 to 192
- cache_keys: bfloat16 [65536, 2048], P('seq', 'head'), may hold values from -6 to 6
- cache_values: bfloat16 [65536, 2048], P('seq', 'head'), may hold values from -12 to 12
- choices: int32 [2048, 3], P('seq'), may hold values from 0 to 127, as said below
Outputs:
- grad_queries: bfloat16 [16384, 2048], P('seq', 'head')
- grad_new_keys: bfloat16 [16384, 2048], P('seq', 'head')
- grad_new_values: bfloat16 [16384, 2048], P('seq', 'head')
- grad_cache_keys: bfloat16 [65536, 2048], P('seq', 'head')
- grad_cache_values: bfloat16 [65536, 2048], P('seq', 'head')
The draws below stay inside these ranges and needn't reach their ends.
Inputs may be any that keep to these rules, and one draw needn't show every extreme that they name: `choices`: each row names 3 different blocks. Among the spans of one block of new tokens no cached block is named more than 1 times, and some cached block exactly 1 times.
All inputs are finite; a program needn't handle non-finite values.
Results may differ from the reference program's by a relative error of at most 0.007.
Values may be sent and summed in bfloat16 or wider, within the bound.
A program may use at most 64 MiB of HBM per device.

```python
import math
import jax
import jax.numpy as jnp
from jax import lax

HEADS = 16
DH = 128
BLK = 512
SPAN = 8
TOPK = 3
QBLOCK = 128
CTX = 65536
TOTQ = 16384
N_SEQ = 128


def draw_queries(key, part):
    key = jax.random.fold_in(key, 1)
    row_count = QBLOCK * N_SEQ
    feature_count = HEADS * DH
    result = jax.random.truncated_normal(key, -4.5, 4.5, (row_count, feature_count), jnp.float32)
    return result.astype(jnp.bfloat16)


def draw_new_keys(key, part):
    key = jax.random.fold_in(key, 2)
    row_count = QBLOCK * N_SEQ
    feature_count = HEADS * DH
    result = jax.random.truncated_normal(key, -4.5, 4.5, (row_count, feature_count), jnp.float32)
    return result.astype(jnp.bfloat16)


def draw_choices(key, part):
    key = jax.random.fold_in(key, 3)
    blocks = N_SEQ
    per_dev = QBLOCK // SPAN
    popular_count = max(1, blocks // 16)
    popular = (jax.random.permutation(jax.random.fold_in(key, 1), blocks) < popular_count).astype(jnp.int32)

    def one_device(dev_key):
        jitter = jax.random.randint(jax.random.fold_in(dev_key, 1), (blocks,), 0, 65536)
        ranking = (jitter + popular * 65536) * blocks + jnp.arange(blocks, dtype=jnp.int32)
        block_order = jnp.argsort(-ranking)
        span_order = jax.random.permutation(jax.random.fold_in(dev_key, 2), per_dev)
        slot_index = span_order[:, None] * TOPK + jnp.arange(TOPK)[None, :]
        return block_order[slot_index % blocks]
    device_keys = jax.random.split(jax.random.fold_in(key, 2), N_SEQ)
    return jax.vmap(one_device)(device_keys).reshape(N_SEQ * per_dev, TOPK).astype(jnp.int32)


def block_levels(stream_key, dims, cuts, smallest, high):
    def one(axis_at, parts):
        steps = jax.random.uniform(jax.random.fold_in(jax.random.fold_in(stream_key, 6), axis_at), (parts,), jnp.float32, smallest / len(cuts), high / len(cuts))
        return jnp.repeat(jnp.exp(steps), dims[axis_at] // parts).reshape((-1,) + (1,) * (len(dims) - axis_at - 1))

    loudness = one(*cuts[0])
    for cut in cuts[1:]:
        loudness = loudness * one(*cut)
    return loudness


def scatter_about(key, shape, width, most, cuts=(), kind=jnp.bfloat16):
    values = width * jax.random.normal(key, shape, jnp.float32)
    if cuts:
        values = values * block_levels(key, shape, cuts, -0.22, 0.18)
    return jnp.clip(values, -most, most).astype(kind)


def setup_inputs(seed: int = 0) -> dict:
    seeds = jax.random.split(jax.random.key(seed), 8)
    queries = draw_queries(jax.random.fold_in(seeds[7], 71), 0)
    new_keys = draw_new_keys(jax.random.fold_in(seeds[7], 71), 0)
    new_values = scatter_about(seeds[2], (TOTQ, HEADS * DH), 2.0, 12.0, ((0, 256),))
    grad_out = scatter_about(seeds[3], (TOTQ, HEADS * DH), 32.0, 192.0, ((0, 256),))
    cache_keys = scatter_about(seeds[4], (CTX, HEADS * DH), 1.0, 6.0, ((0, 128), (1, 2)))
    cache_values = scatter_about(seeds[5], (CTX, HEADS * DH), 2.0, 12.0, ((0, 128), (1, 2)))
    choices = draw_choices(jax.random.fold_in(seeds[7], 71), 0)
    return {"queries": queries, "new_keys": new_keys, "new_values": new_values, "grad_out": grad_out, "cache_keys": cache_keys, "cache_values": cache_values, "choices": choices}


def reference(queries, new_keys, new_values, grad_out, cache_keys, cache_values, choices):
    features = HEADS * DH
    scaling = 1.0 / math.sqrt(DH)
    per_segment = QBLOCK // SPAN
    key_count = QBLOCK + TOPK * BLK
    key_places = jnp.concatenate([jnp.arange(QBLOCK, dtype=jnp.int32), jnp.full((TOPK * BLK,), -1, jnp.int32)])
    query_places = jnp.arange(per_segment, dtype=jnp.int32)[:, None] * SPAN + jnp.arange(SPAN, dtype=jnp.int32)[None, :]
    visible = key_places[None, None, :] <= query_places[:, :, None]

    def block_rows(table, block_index):
        return lax.dynamic_slice_in_dim(table, (block_index * BLK).astype(jnp.int32), BLK, 0)

    def segment_step(running, segment):
        grad_ck, grad_cv, grad_nk, grad_nv = running
        first_row = (segment * QBLOCK).astype(jnp.int32)
        query_rows = lax.dynamic_slice_in_dim(queries, first_row, QBLOCK, 0).astype(jnp.float32).reshape(per_segment, SPAN, HEADS, DH)
        grad_rows = lax.dynamic_slice_in_dim(grad_out, first_row, QBLOCK, 0).astype(jnp.float32).reshape(per_segment, SPAN, HEADS, DH)
        own_keys = lax.dynamic_slice_in_dim(new_keys, first_row, QBLOCK, 0)
        own_values = lax.dynamic_slice_in_dim(new_values, first_row, QBLOCK, 0)
        picked = lax.dynamic_slice_in_dim(choices, (segment * per_segment).astype(jnp.int32), per_segment, 0)
        flat_picks = picked.reshape(-1).astype(jnp.int32)
        gathered_keys = jax.vmap(lambda block_index: block_rows(cache_keys, block_index))(flat_picks).reshape(per_segment, TOPK * BLK, features)
        gathered_values = jax.vmap(lambda block_index: block_rows(cache_values, block_index))(flat_picks).reshape(per_segment, TOPK * BLK, features)
        all_keys = jnp.concatenate([jnp.broadcast_to(own_keys[None], (per_segment, QBLOCK, features)), gathered_keys], axis=1)
        all_keys = all_keys.astype(jnp.float32).reshape(per_segment, key_count, HEADS, DH)
        all_values = jnp.concatenate([jnp.broadcast_to(own_values[None], (per_segment, QBLOCK, features)), gathered_values], axis=1)
        all_values = all_values.astype(jnp.float32).reshape(per_segment, key_count, HEADS, DH)
        scores = jnp.einsum('crhd,ckhd->chrk', query_rows, all_keys) * scaling
        scores = jnp.where(visible[:, None], scores, -jnp.inf)
        highest = lax.optimization_barrier(jnp.max(scores, axis=3, keepdims=True))
        log_norm = highest + jnp.log(lax.optimization_barrier(jnp.sum(jnp.exp(scores - highest), axis=3, keepdims=True)))
        weights = jnp.exp(scores - log_norm)
        grad_weights = jnp.einsum('crhd,ckhd->chrk', grad_rows, all_values)
        deltas = lax.optimization_barrier(jnp.sum(weights * grad_weights, axis=3, keepdims=True))
        grad_scores = weights * (grad_weights - deltas)
        weights_low = lax.optimization_barrier(weights.astype(jnp.bfloat16)).astype(jnp.float32)
        grad_low = lax.optimization_barrier(grad_scores.astype(jnp.bfloat16)).astype(jnp.float32)
        own_query = jnp.einsum('chrk,ckhd->crhd', grad_low[..., :QBLOCK], all_keys[:, :QBLOCK]) * scaling
        gated_low = grad_low[..., QBLOCK:].reshape(per_segment, HEADS, SPAN, TOPK, BLK)
        gated_keys = all_keys[:, QBLOCK:].reshape(per_segment, TOPK, BLK, HEADS, DH)
        gated_query = jnp.einsum('chrtk,ctkhd->ctrhd', gated_low, gated_keys) * scaling
        gated_query = lax.optimization_barrier(gated_query.astype(jnp.bfloat16)).astype(jnp.float32)
        grad_query = own_query + lax.optimization_barrier(jnp.sum(gated_query, axis=1))
        grad_keys = jnp.einsum('chrk,crhd->ckhd', grad_low, query_rows) * scaling
        grad_values = jnp.einsum('chrk,crhd->ckhd', weights_low, grad_rows)
        grad_keys = grad_keys.reshape(per_segment, key_count, features)
        grad_values = grad_values.reshape(per_segment, key_count, features)
        own_gk = lax.optimization_barrier(jnp.sum(grad_keys[:, :QBLOCK], axis=0))
        own_gv = lax.optimization_barrier(jnp.sum(grad_values[:, :QBLOCK], axis=0))
        grad_nk = lax.dynamic_update_slice_in_dim(grad_nk, own_gk, first_row, 0)
        grad_nv = lax.dynamic_update_slice_in_dim(grad_nv, own_gv, first_row, 0)
        cache_gk = grad_keys[:, QBLOCK:].reshape(per_segment * TOPK, BLK, features)
        cache_gv = grad_values[:, QBLOCK:].reshape(per_segment * TOPK, BLK, features)

        def add_block(pick_index, partial_sums):
            sum_keys, sum_values = partial_sums
            first_key = (flat_picks[pick_index] * BLK).astype(jnp.int32)
            sum_keys = lax.dynamic_update_slice_in_dim(sum_keys, lax.dynamic_slice_in_dim(sum_keys, first_key, BLK, 0) + cache_gk[pick_index], first_key, 0)
            sum_values = lax.dynamic_update_slice_in_dim(sum_values, lax.dynamic_slice_in_dim(sum_values, first_key, BLK, 0) + cache_gv[pick_index], first_key, 0)
            return (sum_keys, sum_values)
        grad_ck, grad_cv = lax.fori_loop(0, per_segment * TOPK, add_block, (grad_ck, grad_cv))
        query_out = grad_query.reshape(QBLOCK, features).astype(jnp.bfloat16)
        return ((grad_ck, grad_cv, grad_nk, grad_nv), query_out)
    start_state = (jnp.zeros((CTX, features), jnp.float32), jnp.zeros((CTX, features), jnp.float32), jnp.zeros((TOTQ, features), jnp.float32), jnp.zeros((TOTQ, features), jnp.float32))
    final_state, query_grads = lax.scan(segment_step, start_state, jnp.arange(N_SEQ, dtype=jnp.int32))
    grad_ck, grad_cv, grad_nk, grad_nv = final_state
    grad_queries = query_grads.reshape(TOTQ, features)
    return (grad_queries, grad_nk.astype(jnp.bfloat16), grad_nv.astype(jnp.bfloat16), grad_ck.astype(jnp.bfloat16), grad_cv.astype(jnp.bfloat16))
```

```python
import functools
import math

import jax
import jax.numpy as jnp
from jax import lax
from jax.experimental import pallas as pl
from jax.experimental.pallas import tpu as pltpu
from jax.sharding import PartitionSpec as P

DH = 128
SPAN = 8
TOPK = 3
NZ = 8
NX = 4
NY = 4
PLANE = NX * NY
SPANS = 16
FEATS = 1024
HEADS = FEATS // DH
ROWS = SPANS * SPAN
MESH = pl.DeviceIdType.MESH
OFFSETS = (0, -1, 1, -2, 2, -3, 3, 4)
GROUP_OF = (0, 2, 4, 6, 7, 5, 3, 1)


def dispatch_kernel(
    q_ref, g_ref, k_ref, v_ref, tab_ref,
    rbuf, qrows, grows, krows, vrows,
    zbufs, sbuf, tabz, tab_smem,
    head_send, head_recv, local_sem, tab_send, tab_recv, ring_send, ring_recv,
    plane_send, plane_recv,
):
    seq = lax.axis_index("seq")
    head = lax.axis_index("head")
    z = seq // PLANE
    t0 = seq % PLANE
    x0 = t0 // NY
    y0 = t0 % NY

    def z_peer(d):
        return (((z + d) % NZ) * PLANE + t0, head)

    def plane_of(o):
        return ((x0 + o // NY) % NX) * NY + (y0 + o % NY) % NY

    sibling = (seq, 1 - head)
    barrier = pltpu.get_barrier_semaphore()
    pl.semaphore_signal(barrier, inc=1, device_id=sibling, device_id_type=MESH)
    for d in range(1, NZ):
        pl.semaphore_signal(barrier, inc=1, device_id=z_peer(d), device_id_type=MESH)

    def greet(o, carry):
        pl.semaphore_signal(
            barrier, inc=1, device_id=(z * PLANE + plane_of(o), head), device_id_type=MESH
        )
        return carry

    lax.fori_loop(1, PLANE, greet, 0)
    pl.semaphore_wait(barrier, 1 + (NZ - 1) + (PLANE - 1))

    half = ROWS // 2
    my_rows = pl.ds(pl.multiple_of(head * half, half), half)
    my_cols = pl.ds(pl.multiple_of(head * FEATS, FEATS), FEATS)
    other_cols = pl.ds(pl.multiple_of((1 - head) * FEATS, FEATS), FEATS)
    swaps, locals_ = [], []
    for i, (src, dst) in enumerate(
        ((q_ref, qrows), (g_ref, grows), (k_ref, krows), (v_ref, vrows))
    ):
        swap = pltpu.make_async_remote_copy(
            src_ref=src.at[:, other_cols], dst_ref=dst.at[my_rows, :],
            send_sem=head_send.at[i], recv_sem=head_recv.at[i],
            device_id=sibling, device_id_type=MESH,
        )
        swap.start()
        swaps.append(swap)
        keep = pltpu.make_async_copy(src.at[:, my_cols], dst.at[my_rows, :], local_sem.at[i])
        keep.start()
        locals_.append(keep)
    tabs = []
    for d in range(1, NZ):
        tab = pltpu.make_async_remote_copy(
            src_ref=tab_ref.at[(z + d) % NZ], dst_ref=tabz.at[GROUP_OF[(-d) % NZ]],
            send_sem=tab_send.at[d], recv_sem=tab_recv.at[GROUP_OF[(-d) % NZ]],
            device_id=z_peer(d), device_id_type=MESH,
        )
        tab.start()
        tabs.append(tab)
    tabz[0] = tab_ref[z]
    for j in range(NZ):
        zbufs[j][SPANS] = jnp.zeros((2 * SPAN, FEATS), jnp.bfloat16)

    for i in (0, 1):
        locals_[i].wait()
        swaps[i].wait_recv()

    def pack(i, carry):
        rows = pl.ds(pl.multiple_of(2 * SPAN * i, 2 * SPAN), 2 * SPAN)
        qpair = qrows[rows, :].astype(jnp.float32)
        gpair = grows[rows, :].astype(jnp.float32)
        zbufs[0][2 * i] = jnp.concatenate([qpair[:SPAN], gpair[:SPAN]], axis=0).astype(jnp.bfloat16)
        zbufs[0][2 * i + 1] = jnp.concatenate([qpair[SPAN:], gpair[SPAN:]], axis=0).astype(
            jnp.bfloat16
        )
        return carry

    lax.fori_loop(0, SPANS // 2, pack, 0)

    def ring(direction, step):
        src_j = 0 if step == 1 else 2 * (step - 1) - 1 + direction
        dst_j = 7 if step == 4 else 2 * step - 1 + direction
        lo, n = (direction * (SPANS // 2), SPANS // 2) if step == 4 else (0, SPANS)
        return pltpu.make_async_remote_copy(
            src_ref=zbufs[src_j].at[pl.ds(lo, n)], dst_ref=zbufs[dst_j].at[pl.ds(lo, n)],
            send_sem=ring_send.at[direction, step - 1], recv_sem=ring_recv.at[direction, step - 1],
            device_id=z_peer(1 if direction == 0 else -1), device_id_type=MESH,
        )

    rings = {(1, d): ring(d, 1) for d in range(2)}
    for d in range(2):
        rings[1, d].start()

    for tab in tabs:
        tab.wait_recv()
    fetch = pltpu.make_async_copy(tabz, tab_smem, local_sem.at[4])
    fetch.start()
    fetch.wait()

    def spread(j):
        def one(o, carry):
            t = plane_of(o)
            sbuf[j, o - 1] = zbufs[j][tab_smem[j, 0, t]]
            pltpu.make_async_remote_copy(
                src_ref=sbuf.at[j, o - 1], dst_ref=rbuf.at[j, t0],
                send_sem=plane_send.at[j], recv_sem=plane_recv.at[j],
                device_id=(z * PLANE + t, head), device_id_type=MESH,
            ).start()
            return carry

        lax.fori_loop(1, PLANE, one, 0)
        rbuf[j, t0] = zbufs[j][tab_smem[j, 0, t0]]

    spread(0)
    for step in range(1, 5):
        for d in range(2):
            rings[step, d].wait_recv()
            if step < 4:
                rings[step + 1, d] = ring(d, step + 1)
                rings[step + 1, d].start()
        if step < 4:
            spread(2 * step - 1)
            spread(2 * step)
        else:
            spread(7)

    for j in range(NZ):
        arrived = rbuf.at[j, pl.ds(0, PLANE - 1)]
        pltpu.make_async_copy(arrived, arrived, plane_recv.at[j]).wait()
        sent = sbuf.at[j]
        pltpu.make_async_copy(sent, sent, plane_send.at[j]).wait()
    for pending in rings.values():
        pending.wait_send()
    for tab in tabs:
        tab.wait_send()
    for i in (2, 3):
        locals_[i].wait()
        swaps[i].wait_recv()
    for swap in swaps:
        swap.wait_send()


def dispatch(queries, grad_out, new_keys, new_values, table):
    rows = jax.ShapeDtypeStruct((ROWS, FEATS), jnp.bfloat16)
    vmem = pl.BlockSpec(memory_space=pltpu.VMEM)
    hbm = pl.BlockSpec(memory_space=pl.ANY)
    dma = pltpu.SemaphoreType.DMA
    return pl.pallas_call(
        dispatch_kernel,
        out_shape=(
            jax.ShapeDtypeStruct((NZ, PLANE, 2 * SPAN, FEATS), jnp.bfloat16), rows, rows, rows, rows,
        ),
        in_specs=[hbm, hbm, hbm, hbm, vmem],
        out_specs=(vmem,) * 5,
        scratch_shapes=[
            [pltpu.VMEM((SPANS + 1, 2 * SPAN, FEATS), jnp.bfloat16)] * NZ,
            pltpu.VMEM((NZ, PLANE - 1, 2 * SPAN, FEATS), jnp.bfloat16),
            pltpu.VMEM((NZ, SPAN, 128), jnp.int32),
            pltpu.SMEM((NZ, SPAN, 128), jnp.int32),
            dma((4,)), dma((4,)), dma((5,)), dma((NZ,)), dma((NZ,)), dma((2, 4)), dma((2, 4)),
            dma((NZ,)), dma((NZ,)),
        ],
        compiler_params=pltpu.CompilerParams(
            collective_id=0, has_side_effects=True, vmem_limit_bytes=40 * 1024 * 1024
        ),
    )(queries, grad_out, new_keys, new_values, table)


def block_stats(query_tile, grad_tile, key_rows, value_rows, scaling, causal_mask):
    scores = (
        jnp.einsum("rhd,khd->hrk", query_tile, key_rows, preferred_element_type=jnp.float32)
        * scaling
    )
    if causal_mask is not None:
        scores = jnp.where(causal_mask[None], scores, -jnp.inf)
    highest = jnp.max(scores, axis=2)
    weights = jnp.exp(scores - highest[:, :, None])
    totals = jnp.sum(weights, axis=2)
    grad_weights = jnp.einsum(
        "rhd,khd->hrk", grad_tile, value_rows, preferred_element_type=jnp.float32
    )
    inners = jnp.sum(weights * grad_weights, axis=2)
    return (highest + jnp.log(totals)).T, (inners / totals).T


def block_grads(
    query_tile, grad_tile, key_rows, value_rows, log_norm, deltas, scaling, causal_mask
):
    scores = (
        jnp.einsum("rhd,khd->hrk", query_tile, key_rows, preferred_element_type=jnp.float32)
        * scaling
    )
    if causal_mask is not None:
        scores = jnp.where(causal_mask[None], scores, -jnp.inf)
    weights = jnp.exp(scores - log_norm.T[:, :, None])
    grad_weights = jnp.einsum(
        "rhd,khd->hrk", grad_tile, value_rows, preferred_element_type=jnp.float32
    )
    grad_scores = weights * (grad_weights - deltas.T[:, :, None])
    weights_low = weights.astype(jnp.bfloat16)
    grad_low = grad_scores.astype(jnp.bfloat16)
    grad_query = (
        jnp.einsum("hrk,khd->rhd", grad_low, key_rows, preferred_element_type=jnp.float32) * scaling
    )
    grad_keys = (
        jnp.einsum("hrk,rhd->khd", grad_low, query_tile, preferred_element_type=jnp.float32)
        * scaling
    )
    grad_values = jnp.einsum(
        "hrk,rhd->khd", weights_low, grad_tile, preferred_element_type=jnp.float32
    )
    return (grad_query, grad_keys, grad_values)


def body(queries, new_keys, new_values, grad_out, cache_keys, cache_values, choices):
    devices = lax.axis_size("seq")
    z = lax.axis_index("seq") // PLANE
    scaling = 1.0 / math.sqrt(DH)
    flat_picks = choices.reshape(-1)
    hits = choices[:, :, None] == jnp.arange(devices, dtype=jnp.int32)[None, None, :]
    span_ids = jnp.arange(SPANS, dtype=jnp.int32)[:, None, None]
    span_for = jnp.min(jnp.where(hits, span_ids, SPANS), axis=(0, 1))
    table = jnp.pad(span_for.reshape(NZ, 1, PLANE), ((0, 0), (0, 0), (0, 128 - PLANE)))
    table = jnp.broadcast_to(table, (NZ, SPAN, 128))
    received, query_rows, grad_rows, own_keys, own_values = dispatch(
        queries, grad_out, new_keys, new_values, table
    )
    work_query = received[:, :, :SPAN].reshape(devices * SPAN, HEADS, DH)
    work_grad = received[:, :, SPAN:].reshape(devices * SPAN, HEADS, DH)
    key_rows = cache_keys.reshape(-1, HEADS, DH)
    value_rows = cache_values.reshape(-1, HEADS, DH)
    to_sources = jnp.asarray(GROUP_OF, jnp.int32)[(jnp.arange(NZ, dtype=jnp.int32) - z) % NZ]
    to_groups = (z + jnp.asarray(OFFSETS, jnp.int32)) % NZ

    def regroup(slots, order):
        return jnp.take(slots.reshape(NZ, -1), order, axis=0).reshape(slots.shape)

    def exchange(slots):
        return lax.all_to_all(slots, "seq", split_axis=0, concat_axis=0, tiled=True)

    def per_pick(returned):
        return jnp.take(returned, flat_picks, axis=0).reshape(SPANS, TOPK, SPAN, -1)

    block_log, block_delta = block_stats(
        work_query, work_grad, key_rows, value_rows, scaling, None
    )
    stats = jnp.concatenate([block_log, block_delta], axis=1).reshape(devices, SPAN, 2 * HEADS)
    pick_stats = per_pick(exchange(regroup(stats, to_sources)))
    places = jnp.arange(ROWS, dtype=jnp.int32)
    causal = places[None, :] <= places[:, None]
    own_query = query_rows.reshape(ROWS, HEADS, DH)
    own_grad = grad_rows.reshape(ROWS, HEADS, DH)
    own_key_rows = own_keys.reshape(ROWS, HEADS, DH)
    own_value_rows = own_values.reshape(ROWS, HEADS, DH)
    own_log, own_delta = block_stats(
        own_query, own_grad, own_key_rows, own_value_rows, scaling, causal
    )
    logs = jnp.concatenate(
        [own_log.reshape(SPANS, 1, SPAN, HEADS), pick_stats[..., :HEADS]], axis=1
    )
    shares = jnp.concatenate(
        [own_delta.reshape(SPANS, 1, SPAN, HEADS), pick_stats[..., HEADS:]], axis=1
    )
    peak = jnp.max(logs, axis=1)
    log_norm = peak + jnp.log(jnp.sum(jnp.exp(logs - peak[:, None]), axis=1))
    deltas = jnp.sum(shares * jnp.exp(logs - log_norm[:, None]), axis=1)
    joint = jnp.concatenate([log_norm, deltas], axis=2)
    joint_slots = jnp.take(
        jnp.pad(joint, ((0, 1), (0, 0), (0, 0))), span_for, axis=0
    )
    work_joint = regroup(exchange(joint_slots), to_groups).reshape(devices * SPAN, 2 * HEADS)
    grad_slots, sum_keys, sum_values = block_grads(
        work_query, work_grad, key_rows, value_rows, work_joint[:, :HEADS], work_joint[:, HEADS:],
        scaling, None,
    )
    grad_slots = grad_slots.astype(jnp.bfloat16).reshape(devices, SPAN, FEATS)
    pick_grads = per_pick(exchange(regroup(grad_slots, to_sources)))
    own_gq, own_gk, own_gv = block_grads(
        own_query, own_grad, own_key_rows, own_value_rows,
        log_norm.reshape(ROWS, HEADS), deltas.reshape(ROWS, HEADS), scaling, causal,
    )
    pick_sum = jnp.sum(pick_grads.astype(jnp.float32), axis=1).reshape(ROWS, FEATS)
    grad_queries = (own_gq.reshape(ROWS, FEATS) + pick_sum).astype(jnp.bfloat16)
    return (
        grad_queries,
        own_gk.reshape(ROWS, FEATS).astype(jnp.bfloat16),
        own_gv.reshape(ROWS, FEATS).astype(jnp.bfloat16),
        sum_keys.reshape(-1, FEATS).astype(jnp.bfloat16),
        sum_values.reshape(-1, FEATS).astype(jnp.bfloat16),
    )


def solution(mesh):
    rows = P(("seq", "head"), None)
    both = P("seq", "head")
    return jax.shard_map(
        body,
        mesh=mesh,
        in_specs=(rows, rows, rows, rows, both, both, P("seq", None)),
        out_specs=(both,) * 5,
        check_vma=False,
    )
```

```python
import math

import jax
import jax.numpy as jnp
from jax import lax
from jax.experimental import pallas as pl
from jax.experimental.pallas import tpu as pltpu
from jax.sharding import PartitionSpec as P

DH = 128
SPAN = 8
TOPK = 3
NZ = 8
NX = 4
NY = 4
PLANE = NX * NY
SPANS = 16
FEATS = 1024
HEADS = FEATS // DH
ROWS = SPANS * SPAN
BLK = 512
PAIRS = NZ // 2
PAIR_ROWS = 2 * PLANE * SPAN
UNIT = 2 * SPAN
CHUNKS = 4
CHUNK = SPANS // CHUNKS
SCALING = 1.0 / math.sqrt(DH)
LOG2E = math.log2(math.e)
SCALING2 = SCALING * LOG2E
MESH = pl.DeviceIdType.MESH
OFFSETS = (-1, 1, -2, 2, -3, 3, 0, 4)
GROUP_OF = (6, 1, 3, 5, 7, 4, 2, 0)
OWN = 6
FAR = 7
TAB_A, TAB_B, TAB_S, TAB_END = 0, 256, 384, 512
BF16 = jnp.bfloat16
F32 = jnp.float32
HIGHEST = lax.Precision.HIGHEST


def iota(shape, axis):
    return lax.broadcasted_iota(jnp.int32, shape, axis)


def nt(a, b, precision=None):
    return lax.dot_general(
        a, b, (((1,), (1,)), ((), ())), precision=precision, preferred_element_type=F32
    )


def tn(a, b, precision=None):
    return lax.dot_general(
        a, b, (((0,), (0,)), ((), ())), precision=precision, preferred_element_type=F32
    )


def nn(a, b, precision=None):
    return jnp.dot(a, b, precision=precision, preferred_element_type=F32)


def lane_mask(lanes):
    return iota((128, lanes), 0) // 16 == iota((128, lanes), 1) % SPAN


def pick_pair(p):
    row, lane = iota((128, PAIR_ROWS), 0), iota((128, PAIR_ROWS), 1)
    hit = (row // NZ == lane // UNIT) & (row % NZ == 2 * p + (lane // SPAN) % 2)
    return hit.astype(F32)


def pick_own():
    return (iota((SPANS, ROWS), 0) == iota((SPANS, ROWS), 1) // SPAN).astype(F32)


def stacked(stats):
    tall = jnp.concatenate([stats] * SPAN, axis=0)
    return jnp.where(lane_mask(stats.shape[1]), tall, 0.0)


def unstacked(wide):
    kept = jnp.where(lane_mask(wide.shape[1]), wide, 0.0)
    return jnp.sum(kept.reshape(SPAN, 2 * HEADS, wide.shape[1]), axis=0)


def head_cols(h):
    return pl.ds(pl.multiple_of(h * DH, DH), DH)


def kernel(
    q_hbm, g_hbm, k_hbm, v_hbm, ck_hbm, cv_hbm, tab_ref, sel_ref,
    gq_out, gnk_out, gnv_out, gck_hbm, gcv_hbm,
    own_q, own_g, own_k, own_v, kc, vc, kt,
    zbufs, sbuf, rbuf, tabz, tab_smem, qs, gs, wl, gl,
    stat, own_stat, st_out, st_in, zst_out, zst_in, nz, nr_out, nr_in, joint, own_joint,
    gqb, gr, rs_out, rs_in, own_gq, gck, gcv,
    head_send, head_recv, local_sem, tab_send, tab_recv, ring_send, ring_recv,
    plane_send, plane_recv, st_send, st_recv, zst_send, zst_recv, nz_send, nz_recv,
    nr_send, nr_recv, gr_send, gr_recv, rs_send, rs_recv,
):
    seq = lax.axis_index("seq")
    head = lax.axis_index("head")
    z = seq // PLANE
    t0 = seq % PLANE
    x0 = t0 // NY
    y0 = t0 % NY

    def z_peer(d):
        return (((z + d) % NZ) * PLANE + t0, head)

    def plane_of(o):
        return ((x0 + o // NY) % NX) * NY + (y0 + o % NY) % NY

    def plane_peer(t):
        return (z * PLANE + t, head)

    def remote(src, dst, send, recv, device):
        return pltpu.make_async_remote_copy(
            src_ref=src, dst_ref=dst, send_sem=send, recv_sem=recv,
            device_id=device, device_id_type=MESH,
        )

    def await_bytes(ref, sem):
        pltpu.make_async_copy(ref, ref, sem).wait()

    fetch_k = pltpu.make_async_copy(ck_hbm, kc, local_sem.at[5])
    fetch_v = pltpu.make_async_copy(cv_hbm, vc, local_sem.at[6])
    half = ROWS // 2
    my_rows = pl.ds(pl.multiple_of(head * half, half), half)
    my_cols = pl.ds(pl.multiple_of(head * FEATS, FEATS), FEATS)
    other_cols = pl.ds(pl.multiple_of((1 - head) * FEATS, FEATS), FEATS)
    sources = ((q_hbm, own_q), (g_hbm, own_g), (k_hbm, own_k), (v_hbm, own_v))
    keeps = [
        pltpu.make_async_copy(src.at[:, my_cols], dst.at[my_rows, :], local_sem.at[i])
        for i, (src, dst) in enumerate(sources)
    ]
    for keep in keeps:
        keep.start()

    sibling = (seq, 1 - head)
    barrier = pltpu.get_barrier_semaphore()
    pl.semaphore_signal(barrier, inc=1, device_id=sibling, device_id_type=MESH)
    for d in range(1, NZ):
        pl.semaphore_signal(barrier, inc=1, device_id=z_peer(d), device_id_type=MESH)

    def greet(o, carry):
        pl.semaphore_signal(
            barrier, inc=1, device_id=plane_peer(plane_of(o)), device_id_type=MESH
        )
        return carry

    lax.fori_loop(1, PLANE, greet, 0)
    for i in range(NZ):
        zbufs[i][SPANS] = jnp.zeros((UNIT, FEATS), BF16)
    tabz[OWN] = tab_ref[z]
    pl.semaphore_wait(barrier, 1 + (NZ - 1) + (PLANE - 1))

    swaps = [
        remote(src.at[:, other_cols], dst.at[my_rows, :], head_send.at[i], head_recv.at[i], sibling)
        for i, (src, dst) in enumerate(sources)
    ]
    for swap in swaps[:2]:
        swap.start()
    tabs = []
    for d in range(1, NZ):
        i = GROUP_OF[(-d) % NZ]
        tab = remote(tab_ref.at[(z + d) % NZ], tabz.at[i], tab_send.at[d], tab_recv.at[i], z_peer(d))
        tab.start()
        tabs.append(tab)
    for swap in swaps[2:]:
        swap.start()
    fetch_k.start()
    fetch_v.start()
    for i in (0, 1):
        keeps[i].wait()
        swaps[i].wait_recv()

    def pack(i, carry):
        rows = pl.ds(pl.multiple_of(UNIT * i, UNIT), UNIT)
        qpair = own_q[rows, :].astype(F32)
        gpair = own_g[rows, :].astype(F32)
        zbufs[OWN][2 * i] = jnp.concatenate([qpair[:SPAN], gpair[:SPAN]], axis=0).astype(BF16)
        zbufs[OWN][2 * i + 1] = jnp.concatenate([qpair[SPAN:], gpair[SPAN:]], axis=0).astype(BF16)
        return carry

    rings = {}

    def ring(direction, step, chunk):
        src_i = OWN if step == 1 else 2 * (step - 2) + direction
        dst_i = FAR if step == 4 else 2 * (step - 1) + direction
        part = pl.ds(chunk * CHUNK, CHUNK)
        copy = remote(
            zbufs[src_i].at[part], zbufs[dst_i].at[part],
            ring_send.at[direction, step - 1, chunk], ring_recv.at[direction, step - 1, chunk],
            z_peer(1 if direction == 0 else -1),
        )
        copy.start()
        rings[direction, step, chunk] = copy

    for chunk in range(CHUNKS):
        lax.fori_loop(2 * chunk, 2 * chunk + 2, pack, 0)
        for direction in range(2):
            ring(direction, 1, chunk)

    for tab in tabs:
        tab.wait_recv()
    to_smem = pltpu.make_async_copy(
        tabz.at[:, :, pl.ds(TAB_S, TAB_END - TAB_S)], tab_smem, local_sem.at[4]
    )
    to_smem.start()
    to_smem.wait()

    def spread(i):
        def one(o, carry):
            t = plane_of(o)
            sbuf[i, o - 1] = zbufs[i][tab_smem[i, 0, t]]
            remote(
                sbuf.at[i, o - 1], rbuf.at[i, t0], plane_send.at[i], plane_recv.at[i], plane_peer(t)
            ).start()
            return carry

        lax.fori_loop(1, PLANE, one, 0)
        rbuf[i, t0] = zbufs[i][tab_smem[i, 0, t0]]

    def unpack(p):
        for i in (2 * p, 2 * p + 1):
            await_bytes(rbuf.at[i, pl.ds(0, PLANE - 1)], plane_recv.at[i])

        def one(t, carry):
            rows = pl.ds(pl.multiple_of(p * PAIR_ROWS + t * UNIT, UNIT), UNIT)
            a = rbuf[2 * p, t].astype(F32)
            b = rbuf[2 * p + 1, t].astype(F32)
            qs[rows, :] = jnp.concatenate([a[:SPAN], b[:SPAN]], axis=0).astype(BF16)
            gs[rows, :] = jnp.concatenate([a[SPAN:], b[SPAN:]], axis=0).astype(BF16)
            return carry

        lax.fori_loop(0, PLANE, one, 0)

    def pair_rows(p):
        return pl.ds(p * PAIR_ROWS, PAIR_ROWS)

    def first_head(p):
        def one(h, carry):
            cols = head_cols(h)
            scores = nt(kc[:, cols], qs[pair_rows(p), cols]) * SCALING2
            high = jnp.max(scores, axis=0, keepdims=True)
            weights = jnp.exp2(scores - high)
            total = jnp.sum(weights, axis=0, keepdims=True)
            grad_weights = nt(vc[:, cols], gs[pair_rows(p), cols])
            inner = jnp.sum(weights * grad_weights, axis=0, keepdims=True)
            stat[p, pl.ds(h, 1), :] = high + jnp.log(total) * LOG2E
            stat[p, pl.ds(HEADS + h, 1), :] = inner / total
            return carry

        return one

    def own_scores(cols):
        scores = nt(own_k[:, cols], own_q[:, cols]) * SCALING2
        seen = iota((ROWS, ROWS), 0) <= iota((ROWS, ROWS), 1)
        return jnp.where(seen, scores, -jnp.inf)

    def own_first(h, carry):
        cols = head_cols(h)
        scores = own_scores(cols)
        high = jnp.max(scores, axis=0, keepdims=True)
        weights = jnp.exp2(scores - high)
        total = jnp.sum(weights, axis=0, keepdims=True)
        grad_weights = nt(own_v[:, cols], own_g[:, cols])
        inner = jnp.sum(weights * grad_weights, axis=0, keepdims=True)
        own_stat[pl.ds(h, 1), :] = high + jnp.log(total) * LOG2E
        own_stat[pl.ds(HEADS + h, 1), :] = inner / total
        return carry

    def turn_keys(h, carry):
        kt[h] = kc[:, head_cols(h)].T
        return carry

    spread(OWN)
    for i in (2, 3):
        keeps[i].wait()
        swaps[i].wait_recv()
    fetch_k.wait()
    fetch_v.wait()
    for step in range(1, 5):
        if step == 4:
            unpack(1)
        if step == 3:
            unpack(0)
        for chunk in range(CHUNKS):
            for direction in range(2):
                if step == 4 and chunk // 2 != direction:
                    continue
                rings[direction, step, chunk].wait_recv()
                if step < 3 or (step == 3 and chunk // 2 == direction):
                    ring(direction, step + 1, chunk)
            heads = (2 * chunk, 2 * chunk + 2)
            if step == 1:
                lax.fori_loop(*heads, own_first, 0)
            elif step == 2:
                lax.fori_loop(*heads, turn_keys, 0)
            else:
                lax.fori_loop(*heads, first_head(step - 3), 0)
        if step < 4:
            spread(2 * (step - 1))
            spread(2 * (step - 1) + 1)
        else:
            spread(FAR)
    for p in (2, 3):
        unpack(p)
        lax.fori_loop(0, HEADS, first_head(p), 0)

    slot_stats = nt(pick_pair(0), stacked(stat[0]), HIGHEST)
    for p in range(1, PAIRS):
        slot_stats += nt(pick_pair(p), stacked(stat[p]), HIGHEST)
    st_out[...] = slot_stats.reshape(PLANE, NZ, 128)

    def plane_all(out, into, send, recv):
        def one(o, carry):
            t = plane_of(o)
            remote(out.at[t], into.at[t0], send, recv, plane_peer(t)).start()
            return carry

        lax.fori_loop(1, PLANE, one, 0)
        into[t0] = out[t0]

    plane_all(st_out, st_in, st_send.at[0], st_recv.at[0])
    own_slots = nt(pick_own(), stacked(own_stat[...]), HIGHEST)
    row, lane = iota((128, 128), 0), iota((128, 128), 1)
    swap_order = ((row // PLANE == lane % NZ) & (row % PLANE == lane // NZ)).astype(F32)
    await_bytes(st_in.at[pl.ds(0, PLANE - 1)], st_recv.at[0])
    routed = nn(swap_order, st_in[...].reshape(128, 128), HIGHEST)
    zst_out[...] = routed.reshape(NZ, PLANE, 128)
    stats_home = []
    for i in range(NZ):
        j = GROUP_OF[(-OFFSETS[i]) % NZ]
        if i == OWN:
            zst_in[OWN] = zst_out[OWN]
            continue
        copy = remote(
            zst_out.at[i], zst_in.at[j], zst_send.at[i], zst_recv.at[j], z_peer(OFFSETS[i])
        )
        copy.start()
        stats_home.append(copy)
    for copy in stats_home:
        copy.wait_recv()

    chosen = (sel_ref[...] == iota((TOPK * SPANS, 128), 1)).astype(F32)
    picked = nn(chosen, zst_in[...].reshape(128, 128), HIGHEST)
    logs = [own_slots] + [picked[SPANS * t:SPANS * (t + 1)] for t in range(TOPK)]
    peak = jnp.maximum(jnp.maximum(logs[0], logs[1]), jnp.maximum(logs[2], logs[3]))
    shares = [jnp.exp2(log - peak) for log in logs]
    total = (shares[0] + shares[1]) + (shares[2] + shares[3])
    norm = peak + jnp.log(total) * LOG2E
    delta = jnp.zeros((SPANS, 128), F32)
    for share, log in zip(shares, logs):
        delta += pltpu.roll(share / total, HEADS, 1) * log
    is_norm = iota((SPANS, 128), 1) % (2 * HEADS) < HEADS
    nz[OWN] = jnp.where(is_norm, norm, delta)
    norms_out = []
    for d in range(1, NZ):
        i = GROUP_OF[(-d) % NZ]
        copy = remote(nz.at[OWN], nz.at[i], nz_send.at[d], nz_recv.at[i], z_peer(d))
        copy.start()
        norms_out.append(copy)
    own_joint[...] = unstacked(tn(nz[OWN], pick_own(), HIGHEST))
    lane8 = iota((SPANS, 128), 1) % NZ
    span_row = iota((SPANS, 128), 0)
    routes = jnp.concatenate(
        [
            jnp.where((lane8 == i) & (tabz[i, 0:1, TAB_B:TAB_S] == span_row), 1.0, 0.0)
            for i in range(NZ)
        ],
        axis=0,
    ).astype(F32)
    for copy in norms_out:
        copy.wait_recv()
    nr_out[...] = tn(routes, nz[...].reshape(128, 128), HIGHEST).reshape(PLANE, NZ, 128)
    plane_all(nr_out, nr_in, nr_send.at[0], nr_recv.at[0])

    def own_second(h, carry):
        cols = head_cols(h)
        weights = jnp.exp2(own_scores(cols) - own_joint[pl.ds(h, 1), :])
        grad_weights = nt(own_v[:, cols], own_g[:, cols])
        grad_scores = weights * (grad_weights - own_joint[pl.ds(HEADS + h, 1), :])
        weights_low = weights.astype(BF16)
        grad_low = grad_scores.astype(BF16)
        own_gq[:, cols] = tn(grad_low, own_k[:, cols]) * SCALING
        gnk_out[:, cols] = (nn(grad_low, own_q[:, cols]) * SCALING).astype(BF16)
        gnv_out[:, cols] = nn(weights_low, own_g[:, cols]).astype(BF16)
        return carry

    lax.fori_loop(0, HEADS, own_second, 0)
    await_bytes(nr_in.at[pl.ds(0, PLANE - 1)], nr_recv.at[0])

    def second(p):
        joint[p] = unstacked(tn(nr_in[...].reshape(128, 128), pick_pair(p), HIGHEST))

        def one(h, carry):
            cols = head_cols(h)
            scores = nt(kc[:, cols], qs[pair_rows(p), cols]) * SCALING2
            weights = jnp.exp2(scores - joint[p, pl.ds(h, 1), :])
            grad_weights = nt(vc[:, cols], gs[pair_rows(p), cols])
            grad_scores = weights * (grad_weights - joint[p, pl.ds(HEADS + h, 1), :])
            grad_low = grad_scores.astype(BF16)
            wl[h, :, pair_rows(p)] = weights.astype(BF16)
            gl[h, :, pair_rows(p)] = grad_low
            grad_query = (nn(kt[h], grad_low) * SCALING).T
            gqb[p, :, :, cols] = grad_query.reshape(PLANE, UNIT, DH).astype(BF16)
            return carry

        lax.fori_loop(0, HEADS, one, 0)
        plane_all(gqb.at[p], gr.at[p], gr_send.at[p], gr_recv.at[p])

    def arrived(p):
        await_bytes(gr.at[p, pl.ds(0, PLANE - 1)], gr_recv.at[p])

    def span_sums(i, lo, n):
        p, side = i // 2, i % 2
        row, lane = iota((n, PAIR_ROWS), 0) + lo, iota((n, PAIR_ROWS), 1)
        hit = (tabz[i, 0:1, TAB_A:TAB_B] == row // SPAN) & (lane % UNIT == row % SPAN + SPAN * side)
        return nn(jnp.where(hit, 1.0, 0.0).astype(BF16), gr[p].reshape(PAIR_ROWS, FEATS))

    homes = {}

    def home(step):
        for part in range(2):
            for direction in range(2):
                if step == 1 and part != direction:
                    continue
                rows = pl.ds(part * half, half)
                i = FAR if step == 1 else 2 * (4 - step) + 1 - direction
                sums = span_sums(i, part * half, half)
                if (direction, step - 1, part) in homes:
                    homes[direction, step - 1, part].wait_recv()
                    sums += rs_in[direction, step - 2, rows, :].astype(F32)
                rs_out[direction, step - 1, rows, :] = sums.astype(BF16)
                copy = remote(
                    rs_out.at[direction, step - 1, rows, :], rs_in.at[direction, step - 1, rows, :],
                    rs_send.at[direction, step - 1, part], rs_recv.at[direction, step - 1, part],
                    z_peer(1 if direction == 0 else -1),
                )
                copy.start()
                homes[direction, step, part] = copy

    def cache_grads(h, carry):
        cols = head_cols(h)
        gck[:, cols] = (nn(gl[h], qs[:, cols]) * SCALING).astype(BF16)
        gcv[:, cols] = nn(wl[h], gs[:, cols]).astype(BF16)
        return carry

    second(3)
    second(2)
    arrived(3)
    home(1)
    second(1)
    arrived(2)
    home(2)
    second(0)
    arrived(1)
    home(3)
    lax.fori_loop(0, HEADS // 2, cache_grads, 0)
    arrived(0)
    home(4)
    lax.fori_loop(HEADS // 2, HEADS, cache_grads, 0)
    store_k = pltpu.make_async_copy(gck, gck_hbm, local_sem.at[5])
    store_v = pltpu.make_async_copy(gcv, gcv_hbm, local_sem.at[6])
    store_k.start()
    store_v.start()
    for part in range(2):
        rows = pl.ds(part * half, half)
        sums = own_gq[rows, :] + span_sums(OWN, part * half, half)
        for direction in range(2):
            homes[direction, 4, part].wait_recv()
            sums += rs_in[direction, 3, rows, :].astype(F32)
        gq_out[rows, :] = sums.astype(BF16)

    for swap in swaps:
        swap.wait_send()
    for copy in tabs + stats_home + norms_out + list(rings.values()) + list(homes.values()):
        copy.wait_send()
    for i in range(NZ):
        await_bytes(sbuf.at[i], plane_send.at[i])
    await_bytes(st_out.at[pl.ds(0, PLANE - 1)], st_send.at[0])
    await_bytes(nr_out.at[pl.ds(0, PLANE - 1)], nr_send.at[0])
    for p in range(PAIRS):
        await_bytes(gqb.at[p, pl.ds(0, PLANE - 1)], gr_send.at[p])
    store_k.wait()
    store_v.wait()


def run_kernel(queries, grad_out, new_keys, new_values, cache_keys, cache_values, table, picks):
    vmem = pl.BlockSpec(memory_space=pltpu.VMEM)
    hbm = pl.BlockSpec(memory_space=pl.ANY)
    rows = jax.ShapeDtypeStruct((ROWS, FEATS), BF16)
    block = jax.ShapeDtypeStruct((BLK, FEATS), BF16)
    dma = pltpu.SemaphoreType.DMA
    units = (PLANE, UNIT, FEATS)
    return pl.pallas_call(
        kernel,
        out_shape=(rows, rows, rows, block, block),
        in_specs=[hbm] * 6 + [vmem] * 2,
        out_specs=(vmem, vmem, vmem, hbm, hbm),
        scratch_shapes=[
            *[pltpu.VMEM((ROWS, FEATS), BF16)] * 4,
            *[pltpu.VMEM((BLK, FEATS), BF16)] * 2,
            pltpu.VMEM((HEADS, DH, BLK), BF16),
            [pltpu.VMEM((SPANS + 1, UNIT, FEATS), BF16)] * NZ,
            pltpu.VMEM((NZ, PLANE - 1, UNIT, FEATS), BF16),
            pltpu.VMEM((NZ,) + units, BF16),
            pltpu.VMEM((NZ, SPAN, TAB_END), jnp.int32),
            pltpu.SMEM((NZ, SPAN, TAB_END - TAB_S), jnp.int32),
            *[pltpu.VMEM((PAIRS * PAIR_ROWS, FEATS), BF16)] * 2,
            *[pltpu.VMEM((HEADS, BLK, PAIRS * PAIR_ROWS), BF16)] * 2,
            pltpu.VMEM((PAIRS, 2 * HEADS, PAIR_ROWS), F32),
            pltpu.VMEM((2 * HEADS, ROWS), F32),
            *[pltpu.VMEM((PLANE, NZ, 128), F32)] * 2,
            *[pltpu.VMEM((NZ, PLANE, 128), F32)] * 2,
            pltpu.VMEM((NZ, SPANS, 128), F32),
            *[pltpu.VMEM((PLANE, NZ, 128), F32)] * 2,
            pltpu.VMEM((PAIRS, 2 * HEADS, PAIR_ROWS), F32),
            pltpu.VMEM((2 * HEADS, ROWS), F32),
            *[pltpu.VMEM((PAIRS,) + units, BF16)] * 2,
            *[pltpu.VMEM((2, 4, ROWS, FEATS), BF16)] * 2,
            pltpu.VMEM((ROWS, FEATS), F32),
            *[pltpu.VMEM((BLK, FEATS), BF16)] * 2,
            dma((4,)), dma((4,)), dma((7,)),
            dma((NZ,)), dma((NZ,)),
            dma((2, 4, CHUNKS)), dma((2, 4, CHUNKS)),
            dma((NZ,)), dma((NZ,)),
            dma((1,)), dma((1,)), dma((NZ,)), dma((NZ,)),
            dma((NZ,)), dma((NZ,)), dma((1,)), dma((1,)),
            dma((PAIRS,)), dma((PAIRS,)),
            dma((2, 4, 2)), dma((2, 4, 2)),
        ],
        compiler_params=pltpu.CompilerParams(
            collective_id=0, has_side_effects=True, vmem_limit_bytes=60 * 1024 * 1024
        ),
    )(queries, grad_out, new_keys, new_values, cache_keys, cache_values, table, picks)


def body(queries, new_keys, new_values, grad_out, cache_keys, cache_values, choices):
    z = lax.axis_index("seq") // PLANE
    lanes = jnp.concatenate(
        [
            jnp.arange(256, dtype=jnp.int32) // UNIT,
            jnp.arange(128, dtype=jnp.int32) // NZ,
            jnp.arange(128, dtype=jnp.int32) % PLANE,
        ]
    )
    blocks = jnp.arange(NZ, dtype=jnp.int32)[:, None] * PLANE + lanes[None, :]
    hits = choices[:, :, None, None] == blocks[None, None]
    spans = jnp.arange(SPANS, dtype=jnp.int32)[:, None, None, None]
    table = jnp.min(jnp.where(hits, spans, SPANS), axis=(0, 1))
    table = jnp.broadcast_to(table[:, None, :], (NZ, SPAN, TAB_END))
    away = (choices // PLANE - z) % NZ
    group = jnp.where(away == 0, OWN, jnp.where(away < 4, 2 * away - 1, 14 - 2 * away))
    group = jnp.where(away == 4, FAR, group)
    picks = (group * PLANE + choices % PLANE).T.reshape(TOPK * SPANS, 1)
    picks = jnp.broadcast_to(picks, (TOPK * SPANS, 128))
    return run_kernel(
        queries, grad_out, new_keys, new_values, cache_keys, cache_values, table, picks
    )


def solution(mesh):
    rows = P(("seq", "head"), None)
    both = P("seq", "head")
    return jax.shard_map(
        body,
        mesh=mesh,
        in_specs=(rows, rows, rows, rows, both, both, P("seq", None)),
        out_specs=(both,) * 5,
        check_vma=False,
    )
```

```python
import math

import jax
import jax.numpy as jnp
from jax import lax
from jax.experimental import pallas as pl
from jax.experimental.pallas import tpu as pltpu
from jax.sharding import PartitionSpec as P

DH = 128
SPAN = 8
TOPK = 3
NZ = 8
NX = 4
NY = 4
PLANE = NX * NY
SPANS = 16
FEATS = 1024
HEADS = FEATS // DH
ROWS = SPANS * SPAN
BLK = 512
PAIRS = NZ // 2
PAIR_ROWS = 2 * PLANE * SPAN
UNIT = 2 * SPAN
CHUNKS = 4
NC = 2
WIDTH = FEATS // NC
HALF = HEADS // NC
CHUNK = SPANS // CHUNKS
SCALING = 1.0 / math.sqrt(DH)
LOG2E = math.log2(math.e)
SCALING2 = SCALING * LOG2E
MESH = pl.DeviceIdType.MESH
OFFSETS = (-1, 1, -2, 2, -3, 3, 0, 4)
GROUP_OF = (6, 1, 3, 5, 7, 4, 2, 0)
OWN = 6
FAR = 7
TAB_A, TAB_B, TAB_S, TAB_END = 0, 256, 384, 512
BF16 = jnp.bfloat16
F32 = jnp.float32
HIGHEST = lax.Precision.HIGHEST


def iota(shape, axis):
    return lax.broadcasted_iota(jnp.int32, shape, axis)


def nt(a, b, precision=None):
    return lax.dot_general(
        a, b, (((1,), (1,)), ((), ())), precision=precision, preferred_element_type=F32
    )


def tn(a, b, precision=None):
    return lax.dot_general(
        a, b, (((0,), (0,)), ((), ())), precision=precision, preferred_element_type=F32
    )


def nn(a, b, precision=None):
    return jnp.dot(a, b, precision=precision, preferred_element_type=F32)


def lane_mask(lanes):
    return iota((128, lanes), 0) // 16 == iota((128, lanes), 1) % SPAN


def pick_pair(p):
    row, lane = iota((128, PAIR_ROWS), 0), iota((128, PAIR_ROWS), 1)
    hit = (row // NZ == lane // UNIT) & (row % NZ == 2 * p + (lane // SPAN) % 2)
    return hit.astype(F32)


def pick_own():
    return (iota((SPANS, ROWS), 0) == iota((SPANS, ROWS), 1) // SPAN).astype(F32)


def stacked(stats):
    tall = jnp.concatenate([stats] * SPAN, axis=0)
    return jnp.where(lane_mask(stats.shape[1]), tall, 0.0)


def unstacked(wide):
    kept = jnp.where(lane_mask(wide.shape[1]), wide, 0.0)
    return jnp.sum(kept.reshape(SPAN, 2 * HEADS, wide.shape[1]), axis=0)


def head_cols(h):
    return pl.ds(pl.multiple_of(h * DH, DH), DH)


def kernel(
    q_hbm, g_hbm, k_hbm, v_hbm, ck_hbm, cv_hbm, tab_ref, sel_ref,
    gq_hbm, gnk_hbm, gnv_hbm, gck_hbm, gcv_hbm,
    own_q, own_g, own_k, own_v, kc, vc, kt,
    zbufs, sbuf, rbuf, tabz, tab_smem, qs, gs, wl, gl,
    stat, own_stat, st_out, st_in, zst_out, zst_in, nz, nr_out, nr_in, joint, own_joint,
    gqb, gr, rs_out, rs_in, own_gq, gq, gnk, gnv, gck, gcv,
    head_send, head_recv, local_sem, tab_send, tab_recv, ring_send, ring_recv,
    plane_send, plane_recv, st_send, st_recv, zst_send, zst_recv, nz_send, nz_recv,
    nr_send, nr_recv, gr_send, gr_recv, rs_send, rs_recv,
):
    seq = lax.axis_index("seq")
    head = lax.axis_index("head")
    z = seq // PLANE
    t0 = seq % PLANE
    x0 = t0 // NY
    y0 = t0 % NY

    def z_peer(d):
        return (((z + d) % NZ) * PLANE + t0, head)

    def plane_of(o):
        m = (5 * o) % PLANE
        return ((x0 + m // NY) % NX) * NY + (y0 + m % NY) % NY

    def plane_peer(t):
        return (z * PLANE + t, head)

    def remote(src, dst, send, recv, device):
        return pltpu.make_async_remote_copy(
            src_ref=src, dst_ref=dst, send_sem=send, recv_sem=recv,
            device_id=device, device_id_type=MESH,
        )

    def await_bytes(ref, sem):
        pltpu.make_async_copy(ref, ref, sem).wait()

    half = ROWS // 2
    my_rows = pl.ds(pl.multiple_of(head * half, half), half)
    my_cols = pl.ds(pl.multiple_of(head * FEATS, FEATS), FEATS)
    other_cols = pl.ds(pl.multiple_of((1 - head) * FEATS, FEATS), FEATS)
    sources = ((q_hbm, own_q), (g_hbm, own_g), (k_hbm, own_k), (v_hbm, own_v))
    keeps = [
        pltpu.make_async_copy(src.at[:, my_cols], dst.at[my_rows, :], local_sem.at[i])
        for i, (src, dst) in enumerate(sources)
    ]
    for keep in keeps:
        keep.start()
    fetch_k = pltpu.make_async_copy(ck_hbm, kc, local_sem.at[5])
    fetch_v = pltpu.make_async_copy(cv_hbm, vc, local_sem.at[6])
    fetch_k.start()
    fetch_v.start()

    sibling = (seq, 1 - head)
    barrier = pltpu.get_barrier_semaphore()
    pl.semaphore_signal(barrier, inc=1, device_id=sibling, device_id_type=MESH)
    for d in range(1, NZ):
        pl.semaphore_signal(barrier, inc=1, device_id=z_peer(d), device_id_type=MESH)

    def greet(o, carry):
        pl.semaphore_signal(
            barrier, inc=1, device_id=plane_peer(plane_of(o)), device_id_type=MESH
        )
        return carry

    lax.fori_loop(1, PLANE, greet, 0)
    for c in range(NC):
        for i in range(NZ):
            zbufs[c][i][SPANS] = jnp.zeros((UNIT, WIDTH), BF16)
    stat[...] = jnp.zeros(stat.shape, F32)
    own_stat[...] = jnp.zeros(own_stat.shape, F32)
    tabz[OWN] = tab_ref[z]
    pl.semaphore_wait(barrier, 1 + (NZ - 1) + (PLANE - 1))

    swaps = [
        remote(src.at[:, other_cols], dst.at[my_rows, :], head_send.at[i], head_recv.at[i], sibling)
        for i, (src, dst) in enumerate(sources)
    ]
    for swap in swaps[:2]:
        swap.start()
    tabs = []
    for d in range(1, NZ):
        i = GROUP_OF[(-d) % NZ]
        tab = remote(tab_ref.at[(z + d) % NZ], tabz.at[i], tab_send.at[d], tab_recv.at[i], z_peer(d))
        tab.start()
        tabs.append(tab)
    for swap in swaps[2:]:
        swap.start()
    for i in (0, 1):
        keeps[i].wait()
        swaps[i].wait_recv()

    def half_cols(c):
        return pl.ds(c * WIDTH, WIDTH)

    def pack(c):
        def one(i, carry):
            rows = pl.ds(pl.multiple_of(UNIT * i, UNIT), UNIT)
            qpair = own_q[rows, half_cols(c)].astype(F32)
            gpair = own_g[rows, half_cols(c)].astype(F32)
            zbufs[c][OWN][2 * i] = jnp.concatenate([qpair[:SPAN], gpair[:SPAN]], axis=0).astype(BF16)
            zbufs[c][OWN][2 * i + 1] = jnp.concatenate([qpair[SPAN:], gpair[SPAN:]], axis=0).astype(
                BF16
            )
            return carry

        return one

    rings = {}

    def ring(c, direction, step, chunk):
        src_i = OWN if step == 1 else 2 * (step - 2) + direction
        dst_i = FAR if step == 4 else 2 * (step - 1) + direction
        part = pl.ds(chunk * CHUNK, CHUNK)
        copy = remote(
            zbufs[c][src_i].at[part], zbufs[c][dst_i].at[part],
            ring_send.at[c, direction, step - 1, chunk],
            ring_recv.at[c, direction, step - 1, chunk],
            z_peer(1 if direction == 0 else -1),
        )
        copy.start()
        rings[c, direction, step, chunk] = copy

    for chunk in range(CHUNKS):
        lax.fori_loop(2 * chunk, 2 * chunk + 2, pack(0), 0)
        for direction in range(2):
            ring(0, direction, 1, chunk)

    for tab in tabs:
        tab.wait_recv()
    to_smem = pltpu.make_async_copy(
        tabz.at[:, :, pl.ds(TAB_S, TAB_END - TAB_S)], tab_smem, local_sem.at[4]
    )
    to_smem.start()
    to_smem.wait()

    def spread(c, i):
        def one(o, carry):
            t = plane_of(o)
            sbuf[c, i, o - 1] = zbufs[c][i][tab_smem[i, 0, t]]
            remote(
                sbuf.at[c, i, o - 1], rbuf.at[c, i, t0],
                plane_send.at[c, i], plane_recv.at[c, i], plane_peer(t),
            ).start()
            return carry

        lax.fori_loop(1, PLANE, one, 0)
        rbuf[c, i, t0] = zbufs[c][i][tab_smem[i, 0, t0]]

    def pair_rows(p):
        return pl.ds(p * PAIR_ROWS, PAIR_ROWS)

    def first(c, p):
        for i in (2 * p, 2 * p + 1):
            await_bytes(rbuf.at[c, i, pl.ds(0, PLANE - 1)], plane_recv.at[c, i])

        def unpack(t, carry):
            rows = pl.ds(pl.multiple_of(p * PAIR_ROWS + t * UNIT, UNIT), UNIT)
            a = rbuf[c, 2 * p, t].astype(F32)
            b = rbuf[c, 2 * p + 1, t].astype(F32)
            qs[rows, half_cols(c)] = jnp.concatenate([a[:SPAN], b[:SPAN]], axis=0).astype(BF16)
            gs[rows, half_cols(c)] = jnp.concatenate([a[SPAN:], b[SPAN:]], axis=0).astype(BF16)
            return carry

        lax.fori_loop(0, PLANE, unpack, 0)

        def one(k, carry):
            cols = head_cols(HALF * c + k)
            scores = nt(kc[:, cols], qs[pair_rows(p), cols]) * SCALING2
            high = jnp.max(scores, axis=0, keepdims=True)
            weights = jnp.exp2(scores - high)
            total = jnp.sum(weights, axis=0, keepdims=True)
            grad_weights = nt(vc[:, cols], gs[pair_rows(p), cols])
            inner = jnp.sum(weights * grad_weights, axis=0, keepdims=True)
            stat[c, p, pl.ds(k, 1), :] = high + jnp.log(total) * LOG2E
            stat[c, p, pl.ds(HEADS + k, 1), :] = inner / total
            return carry

        lax.fori_loop(0, HALF, one, 0, unroll=HALF)

    def own_scores(cols):
        scores = nt(own_k[:, cols], own_q[:, cols]) * SCALING2
        seen = iota((ROWS, ROWS), 0) <= iota((ROWS, ROWS), 1)
        return jnp.where(seen, scores, -jnp.inf)

    def own_first(c):
        def one(k, carry):
            cols = head_cols(HALF * c + k)
            scores = own_scores(cols)
            high = jnp.max(scores, axis=0, keepdims=True)
            weights = jnp.exp2(scores - high)
            total = jnp.sum(weights, axis=0, keepdims=True)
            grad_weights = nt(own_v[:, cols], own_g[:, cols])
            inner = jnp.sum(weights * grad_weights, axis=0, keepdims=True)
            own_stat[c, pl.ds(k, 1), :] = high + jnp.log(total) * LOG2E
            own_stat[c, pl.ds(HEADS + k, 1), :] = inner / total
            return carry

        return one

    def turn_keys(h, carry):
        kt[h] = kc[:, head_cols(h)].T
        return carry

    def ring_step(c, step, work):
        for chunk in range(CHUNKS):
            for direction in range(2):
                if step == 4 and chunk // 2 != direction:
                    continue
                rings[c, direction, step, chunk].wait_recv()
                if step < 3 or (step == 3 and chunk // 2 == direction):
                    ring(c, direction, step + 1, chunk)
            work(chunk)
        if step < 4:
            spread(c, 2 * (step - 1))
            spread(c, 2 * (step - 1) + 1)
        else:
            spread(c, FAR)

    def plane_all(out, into, send, recv):
        def one(o, carry):
            t = plane_of(o)
            remote(out.at[t], into.at[t0], send, recv, plane_peer(t)).start()
            return carry

        lax.fori_loop(1, PLANE, one, 0)
        into[t0] = out[t0]

    small = []

    def stats_plane(c):
        slots = nt(pick_pair(0), stacked(stat[c, 0]), HIGHEST)
        for p in range(1, PAIRS):
            slots += nt(pick_pair(p), stacked(stat[c, p]), HIGHEST)
        st_out[c] = slots.reshape(PLANE, NZ, 128)
        plane_all(st_out.at[c], st_in.at[c], st_send.at[c], st_recv.at[c])

    stats_home = {}

    def stats_z(c):
        row, lane = iota((128, 128), 0), iota((128, 128), 1)
        swap_order = ((row // PLANE == lane % NZ) & (row % PLANE == lane // NZ)).astype(F32)
        await_bytes(st_in.at[c, pl.ds(0, PLANE - 1)], st_recv.at[c])
        zst_out[c] = nn(swap_order, st_in[c].reshape(128, 128), HIGHEST).reshape(NZ, PLANE, 128)
        stats_home[c] = []
        for i in range(NZ):
            j = GROUP_OF[(-OFFSETS[i]) % NZ]
            if i == OWN:
                zst_in[c, OWN] = zst_out[c, OWN]
                continue
            copy = remote(
                zst_out.at[c, i], zst_in.at[c, j], zst_send.at[c, i], zst_recv.at[c, j],
                z_peer(OFFSETS[i]),
            )
            copy.start()
            stats_home[c].append(copy)
            small.append(copy)

    norms_out = {}

    def norms_z(c):
        own_slots = nt(pick_own(), stacked(own_stat[c]), HIGHEST)
        chosen = (sel_ref[...] == iota((TOPK * SPANS, 128), 1)).astype(F32)
        for copy in stats_home[c]:
            copy.wait_recv()
        picked = nn(chosen, zst_in[c].reshape(128, 128), HIGHEST)
        logs = [own_slots] + [picked[SPANS * t:SPANS * (t + 1)] for t in range(TOPK)]
        peak = jnp.maximum(jnp.maximum(logs[0], logs[1]), jnp.maximum(logs[2], logs[3]))
        shares = [jnp.exp2(log - peak) for log in logs]
        total = (shares[0] + shares[1]) + (shares[2] + shares[3])
        norm = peak + jnp.log(total) * LOG2E
        delta = jnp.zeros((SPANS, 128), F32)
        for share, log in zip(shares, logs):
            delta += pltpu.roll(share / total, HEADS, 1) * log
        is_norm = iota((SPANS, 128), 1) % (2 * HEADS) < HEADS
        nz[c, OWN] = jnp.where(is_norm, norm, delta)
        norms_out[c] = []
        for d in range(1, NZ):
            i = GROUP_OF[(-d) % NZ]
            copy = remote(
                nz.at[c, OWN], nz.at[c, i], nz_send.at[c, d], nz_recv.at[c, i], z_peer(d)
            )
            copy.start()
            norms_out[c].append(copy)
            small.append(copy)
        own_joint[c] = unstacked(tn(nz[c, OWN], pick_own(), HIGHEST))

    def norms_plane(c):
        lane8 = iota((SPANS, 128), 1) % NZ
        span_row = iota((SPANS, 128), 0)
        routes = jnp.concatenate(
            [
                jnp.where((lane8 == i) & (tabz[i, 0:1, TAB_B:TAB_S] == span_row), 1.0, 0.0)
                for i in range(NZ)
            ],
            axis=0,
        ).astype(F32)
        for copy in norms_out[c]:
            copy.wait_recv()
        routed = tn(routes, nz[c].reshape(128, 128), HIGHEST)
        nr_out[c] = routed.reshape(PLANE, NZ, 128)
        plane_all(nr_out.at[c], nr_in.at[c], nr_send.at[c], nr_recv.at[c])

    def norms_arrived(c):
        await_bytes(nr_in.at[c, pl.ds(0, PLANE - 1)], nr_recv.at[c])

    def own_second(c):
        def one(k, carry):
            cols = head_cols(HALF * c + k)
            weights = jnp.exp2(own_scores(cols) - own_joint[c, pl.ds(k, 1), :])
            grad_weights = nt(own_v[:, cols], own_g[:, cols])
            grad_scores = weights * (grad_weights - own_joint[c, pl.ds(HEADS + k, 1), :])
            weights_low = weights.astype(BF16)
            grad_low = grad_scores.astype(BF16)
            own_gq[:, cols] = tn(grad_low, own_k[:, cols]) * SCALING
            gnk[:, cols] = (nn(grad_low, own_q[:, cols]) * SCALING).astype(BF16)
            gnv[:, cols] = nn(weights_low, own_g[:, cols]).astype(BF16)
            return carry

        lax.fori_loop(0, HALF, one, 0, unroll=2)

    def second(c, p):
        joint[c, p] = unstacked(tn(nr_in[c].reshape(128, 128), pick_pair(p), HIGHEST))

        def one(k, carry):
            h = HALF * c + k
            cols = head_cols(h)
            scores = nt(kc[:, cols], qs[pair_rows(p), cols]) * SCALING2
            weights = jnp.exp2(scores - joint[c, p, pl.ds(k, 1), :])
            grad_weights = nt(vc[:, cols], gs[pair_rows(p), cols])
            grad_scores = weights * (grad_weights - joint[c, p, pl.ds(HEADS + k, 1), :])
            grad_low = grad_scores.astype(BF16)
            wl[h, :, pair_rows(p)] = weights.astype(BF16)
            gl[h, :, pair_rows(p)] = grad_low
            grad_query = (nn(kt[h], grad_low) * SCALING).T
            gqb[c, p, :, :, head_cols(k)] = grad_query.reshape(PLANE, UNIT, DH).astype(BF16)
            return carry

        lax.fori_loop(0, HALF, one, 0, unroll=HALF)
        plane_all(gqb.at[c, p], gr.at[c, p], gr_send.at[c, p], gr_recv.at[c, p])

    def arrived(c, p):
        await_bytes(gr.at[c, p, pl.ds(0, PLANE - 1)], gr_recv.at[c, p])

    def span_sums(c, i, lo, n):
        p, side = i // 2, i % 2
        row, lane = iota((n, PAIR_ROWS), 0) + lo, iota((n, PAIR_ROWS), 1)
        hit = (tabz[i, 0:1, TAB_A:TAB_B] == row // SPAN) & (lane % UNIT == row % SPAN + SPAN * side)
        return nn(jnp.where(hit, 1.0, 0.0).astype(BF16), gr[c, p].reshape(PAIR_ROWS, WIDTH))

    homes = {}

    def home(c, step):
        arrived(c, 4 - step)
        for direction in range(2):
            lo, n = (direction * half, half) if step == 1 else (0, ROWS)
            rows = pl.ds(lo, n)
            i = FAR if step == 1 else 2 * (4 - step) + 1 - direction
            sums = span_sums(c, i, lo, n)
            if step == 1:
                rs_out[c, direction, 0, rows, :] = sums.astype(BF16)
            else:
                homes[c, direction, step - 1].wait_recv()
                came = pl.ds(direction * half, half) if step == 2 else rows
                rs_out[c, direction, step - 1] = sums.astype(BF16)
                if step == 2:
                    part = sums[direction * half:(direction + 1) * half]
                else:
                    part = sums
                part += rs_in[c, direction, step - 2, came, :].astype(F32)
                rs_out[c, direction, step - 1, came, :] = part.astype(BF16)
            copy = remote(
                rs_out.at[c, direction, step - 1, rows, :],
                rs_in.at[c, direction, step - 1, rows, :],
                rs_send.at[c, direction, step - 1], rs_recv.at[c, direction, step - 1],
                z_peer(1 if direction == 0 else -1),
            )
            copy.start()
            homes[c, direction, step] = copy

    def cache_grads(c):
        def one(k, carry):
            h = HALF * c + k
            cols = head_cols(h)
            gck[:, cols] = (nn(gl[h], qs[:, cols]) * SCALING).astype(BF16)
            gcv[:, cols] = nn(wl[h], gs[:, cols]).astype(BF16)
            return carry

        lax.fori_loop(0, HALF, one, 0, unroll=2)

    def finish(c):
        sums = own_gq[:, half_cols(c)] + span_sums(c, OWN, 0, ROWS)
        for direction in range(2):
            homes[c, direction, 4].wait_recv()
            sums += rs_in[c, direction, 3].astype(F32)
        gq[:, half_cols(c)] = sums.astype(BF16)

    def nothing(chunk):
        pass

    def own_work(chunk):
        lax.fori_loop(2 * (chunk % 2), 2 * (chunk % 2) + 2, own_first(chunk // 2), 0)

    def turn_work(chunk):
        lax.fori_loop(2 * chunk, 2 * chunk + 2, turn_keys, 0)

    def next_half(chunk):
        lax.fori_loop(2 * chunk, 2 * chunk + 2, pack(1), 0)
        for direction in range(2):
            ring(1, direction, 1, chunk)

    spread(0, OWN)
    for i in (2, 3):
        keeps[i].wait()
        swaps[i].wait_recv()
    fetch_k.wait()
    fetch_v.wait()
    ring_step(0, 1, own_work)
    ring_step(0, 2, turn_work)
    ring_step(0, 3, next_half)
    spread(1, OWN)
    ring_step(0, 4, nothing)
    first(0, 0)
    ring_step(1, 1, nothing)
    first(0, 1)
    ring_step(1, 2, nothing)
    first(0, 2)
    first(0, 3)
    stats_plane(0)
    ring_step(1, 3, nothing)
    stats_z(0)
    ring_step(1, 4, nothing)
    norms_z(0)
    first(1, 0)
    first(1, 1)
    norms_plane(0)
    first(1, 2)
    first(1, 3)
    stats_plane(1)
    norms_arrived(0)
    second(0, 3)
    second(0, 2)
    stats_z(1)
    second(0, 1)
    second(0, 0)
    norms_z(1)
    home(0, 1)
    own_second(0)
    norms_plane(1)
    home(0, 2)
    norms_arrived(1)
    second(1, 3)
    second(1, 2)
    home(0, 3)
    second(1, 1)
    second(1, 0)
    home(0, 4)
    own_second(1)
    store_nk = pltpu.make_async_copy(gnk, gnk_hbm, local_sem.at[0])
    store_nv = pltpu.make_async_copy(gnv, gnv_hbm, local_sem.at[1])
    store_nk.start()
    store_nv.start()
    home(1, 1)
    cache_grads(0)
    home(1, 2)
    cache_grads(1)
    store_k = pltpu.make_async_copy(gck, gck_hbm, local_sem.at[5])
    store_v = pltpu.make_async_copy(gcv, gcv_hbm, local_sem.at[6])
    store_k.start()
    store_v.start()
    home(1, 3)
    home(1, 4)
    finish(0)
    finish(1)
    store_q = pltpu.make_async_copy(gq, gq_hbm, local_sem.at[2])
    store_q.start()

    for copy in swaps + tabs + small + list(rings.values()) + list(homes.values()):
        copy.wait_send()
    for c in range(NC):
        for i in range(NZ):
            await_bytes(sbuf.at[c, i], plane_send.at[c, i])
        await_bytes(st_out.at[c, pl.ds(0, PLANE - 1)], st_send.at[c])
        await_bytes(nr_out.at[c, pl.ds(0, PLANE - 1)], nr_send.at[c])
        for p in range(PAIRS):
            await_bytes(gqb.at[c, p, pl.ds(0, PLANE - 1)], gr_send.at[c, p])
    for store in (store_nk, store_nv, store_k, store_v, store_q):
        store.wait()


def hand_over(*refs):
    made, results, held, (sems,) = refs[:5], refs[5:10], refs[10:15], refs[15:]
    loads = [pltpu.make_async_copy(made[i], held[i], sems.at[0, i]) for i in range(5)]
    stores = [pltpu.make_async_copy(held[i], results[i], sems.at[1, i]) for i in range(5)]
    for load in loads:
        load.start()
    for load, store in zip(loads, stores):
        load.wait()
        store.start()
    for store in stores:
        store.wait()


def run_kernel(queries, grad_out, new_keys, new_values, cache_keys, cache_values, table, picks):
    vmem = pl.BlockSpec(memory_space=pltpu.VMEM)
    hbm = pl.BlockSpec(memory_space=pl.ANY)
    rows = jax.ShapeDtypeStruct((ROWS, FEATS), BF16)
    block = jax.ShapeDtypeStruct((BLK, FEATS), BF16)
    results = (rows, rows, rows, block, block)
    dma = pltpu.SemaphoreType.DMA
    units = (PLANE, UNIT, WIDTH)
    made = pl.pallas_call(
        kernel,
        out_shape=results,
        in_specs=[hbm] * 6 + [vmem] * 2,
        out_specs=(hbm,) * 5,
        scratch_shapes=[
            *[pltpu.VMEM((ROWS, FEATS), BF16)] * 4,
            *[pltpu.VMEM((BLK, FEATS), BF16)] * 2,
            pltpu.VMEM((HEADS, DH, BLK), BF16),
            [[pltpu.VMEM((SPANS + 1, UNIT, WIDTH), BF16)] * NZ] * NC,
            pltpu.VMEM((NC, NZ, PLANE - 1, UNIT, WIDTH), BF16),
            pltpu.VMEM((NC, NZ) + units, BF16),
            pltpu.VMEM((NZ, SPAN, TAB_END), jnp.int32),
            pltpu.SMEM((NZ, SPAN, TAB_END - TAB_S), jnp.int32),
            *[pltpu.VMEM((PAIRS * PAIR_ROWS, FEATS), BF16)] * 2,
            *[pltpu.VMEM((HEADS, BLK, PAIRS * PAIR_ROWS), BF16)] * 2,
            pltpu.VMEM((NC, PAIRS, 2 * HEADS, PAIR_ROWS), F32),
            pltpu.VMEM((NC, 2 * HEADS, ROWS), F32),
            *[pltpu.VMEM((NC, PLANE, NZ, 128), F32)] * 2,
            *[pltpu.VMEM((NC, NZ, PLANE, 128), F32)] * 2,
            pltpu.VMEM((NC, NZ, SPANS, 128), F32),
            *[pltpu.VMEM((NC, PLANE, NZ, 128), F32)] * 2,
            pltpu.VMEM((NC, PAIRS, 2 * HEADS, PAIR_ROWS), F32),
            pltpu.VMEM((NC, 2 * HEADS, ROWS), F32),
            *[pltpu.VMEM((NC, PAIRS) + units, BF16)] * 2,
            *[pltpu.VMEM((NC, 2, 4, ROWS, WIDTH), BF16)] * 2,
            pltpu.VMEM((ROWS, FEATS), F32),
            *[pltpu.VMEM((ROWS, FEATS), BF16)] * 3,
            *[pltpu.VMEM((BLK, FEATS), BF16)] * 2,
            dma((4,)), dma((4,)), dma((7,)),
            dma((NZ,)), dma((NZ,)),
            dma((NC, 2, 4, CHUNKS)), dma((NC, 2, 4, CHUNKS)),
            dma((NC, NZ)), dma((NC, NZ)),
            dma((NC,)), dma((NC,)), dma((NC, NZ)), dma((NC, NZ)),
            dma((NC, NZ)), dma((NC, NZ)), dma((NC,)), dma((NC,)),
            dma((NC, PAIRS)), dma((NC, PAIRS)),
            dma((NC, 2, 4)), dma((NC, 2, 4)),
        ],
        compiler_params=pltpu.CompilerParams(
            collective_id=0, has_side_effects=True, vmem_limit_bytes=60 * 1024 * 1024
        ),
    )(queries, grad_out, new_keys, new_values, cache_keys, cache_values, table, picks)
    return pl.pallas_call(
        hand_over,
        out_shape=results,
        in_specs=[hbm] * 5,
        out_specs=(hbm,) * 5,
        scratch_shapes=[*[pltpu.VMEM(x.shape, BF16) for x in results], dma((2, 5))],
        compiler_params=pltpu.CompilerParams(vmem_limit_bytes=60 * 1024 * 1024),
    )(*made)


def body(queries, new_keys, new_values, grad_out, cache_keys, cache_values, choices):
    z = lax.axis_index("seq") // PLANE
    lanes = jnp.concatenate(
        [
            jnp.arange(256, dtype=jnp.int32) // UNIT,
            jnp.arange(128, dtype=jnp.int32) // NZ,
            jnp.arange(128, dtype=jnp.int32) % PLANE,
        ]
    )
    blocks = jnp.arange(NZ, dtype=jnp.int32)[:, None] * PLANE + lanes[None, :]
    hits = choices[:, :, None, None] == blocks[None, None]
    spans = jnp.arange(SPANS, dtype=jnp.int32)[:, None, None, None]
    table = jnp.min(jnp.where(hits, spans, SPANS), axis=(0, 1))
    table = jnp.broadcast_to(table[:, None, :], (NZ, SPAN, TAB_END))
    away = (choices // PLANE - z) % NZ
    group = jnp.where(away == 0, OWN, jnp.where(away < 4, 2 * away - 1, 14 - 2 * away))
    group = jnp.where(away == 4, FAR, group)
    picks = (group * PLANE + choices % PLANE).T.reshape(TOPK * SPANS, 1)
    picks = jnp.broadcast_to(picks, (TOPK * SPANS, 128))
    return run_kernel(
        queries, grad_out, new_keys, new_values, cache_keys, cache_values, table, picks
    )


def solution(mesh):
    rows = P(("seq", "head"), None)
    both = P("seq", "head")
    return jax.shard_map(
        body,
        mesh=mesh,
        in_specs=(rows, rows, rows, rows, both, both, P("seq", None)),
        out_specs=(both,) * 5,
        check_vma=False,
    )
```

```python
import math

import jax
import jax.numpy as jnp
from jax import lax
from jax.experimental import pallas as pl
from jax.experimental.pallas import tpu as pltpu
from jax.sharding import PartitionSpec as P

DH = 128
SPAN = 8
TOPK = 3
NZ = 8
NX = 4
NY = 4
PLANE = NX * NY
SPANS = 16
FEATS = 1024
HEADS = FEATS // DH
ROWS = SPANS * SPAN
BLK = 512
PAIRS = NZ // 2
PAIR_ROWS = 2 * PLANE * SPAN
UNIT = 2 * SPAN
CHUNKS = 4
NC = 2
WIDTH = FEATS // NC
HALF = HEADS // NC
CHUNK = SPANS // CHUNKS
SCALING = 1.0 / math.sqrt(DH)
LOG2E = math.log2(math.e)
SCALING2 = SCALING * LOG2E
MESH = pl.DeviceIdType.MESH
OFFSETS = (-1, 1, -2, 2, -3, 3, 0, 4)
GROUP_OF = (6, 1, 3, 5, 7, 4, 2, 0)
OWN = 6
FAR = 7
TAB_A, TAB_B, TAB_S, TAB_END = 0, 256, 384, 512
BF16 = jnp.bfloat16
F32 = jnp.float32
HIGHEST = lax.Precision.HIGHEST


def iota(shape, axis):
    return lax.broadcasted_iota(jnp.int32, shape, axis)


def nt(a, b, precision=None):
    return lax.dot_general(
        a, b, (((1,), (1,)), ((), ())), precision=precision, preferred_element_type=F32
    )


def tn(a, b, precision=None):
    return lax.dot_general(
        a, b, (((0,), (0,)), ((), ())), precision=precision, preferred_element_type=F32
    )


def nn(a, b, precision=None):
    return jnp.dot(a, b, precision=precision, preferred_element_type=F32)


def lane_mask(lanes):
    return iota((128, lanes), 0) // 16 == iota((128, lanes), 1) % SPAN


def pick_pair(p):
    row, lane = iota((128, PAIR_ROWS), 0), iota((128, PAIR_ROWS), 1)
    hit = (row // NZ == lane // UNIT) & (row % NZ == 2 * p + (lane // SPAN) % 2)
    return hit.astype(F32)


def pick_own():
    return (iota((SPANS, ROWS), 0) == iota((SPANS, ROWS), 1) // SPAN).astype(F32)


def stacked(stats):
    tall = jnp.concatenate([stats] * SPAN, axis=0)
    return jnp.where(lane_mask(stats.shape[1]), tall, 0.0)


def unstacked(wide):
    kept = jnp.where(lane_mask(wide.shape[1]), wide, 0.0)
    return jnp.sum(kept.reshape(SPAN, 2 * HEADS, wide.shape[1]), axis=0)


def head_cols(h):
    return pl.ds(pl.multiple_of(h * DH, DH), DH)


def kernel(
    q_hbm, g_hbm, k_hbm, v_hbm, ck_hbm, cv_hbm, tab_ref, sel_ref,
    gq_hbm, gnk_hbm, gnv_hbm, gck_hbm, gcv_hbm,
    own_q, own_g, own_k, own_v, kc, vc, kt,
    zbufs, sbuf, rbuf, tab_src, tabz, tab_smem, qs, gs, wl, gl,
    stat, own_stat, st_out, st_in, zst_out, zst_in, nz, nr_out, nr_in, joint, own_joint,
    gqb, gr, rs_out, rs_in, own_gq, gq, gnk, gnv, gck, gcv,
    head_send, head_recv, local_sem, tab_send, tab_recv, ring_send, ring_recv,
    plane_send, plane_recv, st_send, st_recv, zst_send, zst_recv, nz_send, nz_recv,
    nr_send, nr_recv, gr_send, gr_recv, rs_send, rs_recv,
):
    seq = lax.axis_index("seq")
    head = lax.axis_index("head")
    z = seq // PLANE
    t0 = seq % PLANE
    x0 = t0 // NY
    y0 = t0 % NY

    def z_peer(d):
        return (((z + d) % NZ) * PLANE + t0, head)

    def plane_of(o):
        m = (5 * o) % PLANE
        return ((x0 + m // NY) % NX) * NY + (y0 + m % NY) % NY

    def plane_peer(t):
        return (z * PLANE + t, head)

    def remote(src, dst, send, recv, device):
        return pltpu.make_async_remote_copy(
            src_ref=src, dst_ref=dst, send_sem=send, recv_sem=recv,
            device_id=device, device_id_type=MESH,
        )

    def await_bytes(ref, sem):
        pltpu.make_async_copy(ref, ref, sem).wait()

    half = ROWS // 2
    my_rows = pl.ds(pl.multiple_of(head * half, half), half)
    my_cols = pl.ds(pl.multiple_of(head * FEATS, FEATS), FEATS)
    other_cols = pl.ds(pl.multiple_of((1 - head) * FEATS, FEATS), FEATS)
    sources = ((q_hbm, own_q), (g_hbm, own_g), (k_hbm, own_k), (v_hbm, own_v))
    keeps = [
        pltpu.make_async_copy(src.at[:, my_cols], dst.at[my_rows, :], local_sem.at[i])
        for i, (src, dst) in enumerate(sources)
    ]
    for keep in keeps:
        keep.start()
    fetch_k = pltpu.make_async_copy(ck_hbm, kc, local_sem.at[5])
    fetch_v = pltpu.make_async_copy(cv_hbm, vc, local_sem.at[6])
    fetch_k.start()
    fetch_v.start()

    sibling = (seq, 1 - head)
    barrier = pltpu.get_barrier_semaphore()
    pl.semaphore_signal(barrier, inc=1, device_id=sibling, device_id_type=MESH)
    for d in range(1, NZ):
        pl.semaphore_signal(barrier, inc=1, device_id=z_peer(d), device_id_type=MESH)

    def greet(o, carry):
        pl.semaphore_signal(
            barrier, inc=1, device_id=plane_peer(plane_of(o)), device_id_type=MESH
        )
        return carry

    lax.fori_loop(1, PLANE, greet, 0)
    for c in range(NC):
        for i in range(NZ):
            zbufs[c][i][SPANS] = jnp.zeros((UNIT, WIDTH), BF16)
    for plane in range(NZ):
        tab_src[plane] = jnp.broadcast_to(tab_ref[plane:plane + 1, :], (SPAN, TAB_END))
    tabz[OWN] = tab_src[z]
    pl.semaphore_wait(barrier, 1 + (NZ - 1) + (PLANE - 1))

    swaps = [
        remote(src.at[:, other_cols], dst.at[my_rows, :], head_send.at[i], head_recv.at[i], sibling)
        for i, (src, dst) in enumerate(sources)
    ]
    for swap in swaps[:2]:
        swap.start()
    tabs = []
    for d in range(1, NZ):
        i = GROUP_OF[(-d) % NZ]
        tab = remote(tab_src.at[(z + d) % NZ], tabz.at[i], tab_send.at[d], tab_recv.at[i], z_peer(d))
        tab.start()
        tabs.append(tab)
    for swap in swaps[2:]:
        swap.start()
    for i in (0, 1):
        keeps[i].wait()
        swaps[i].wait_recv()

    def half_cols(c):
        return pl.ds(c * WIDTH, WIDTH)

    def pack(c):
        def one(i, carry):
            rows = pl.ds(pl.multiple_of(UNIT * i, UNIT), UNIT)
            qpair = own_q[rows, half_cols(c)].astype(F32)
            gpair = own_g[rows, half_cols(c)].astype(F32)
            zbufs[c][OWN][2 * i] = jnp.concatenate([qpair[:SPAN], gpair[:SPAN]], axis=0).astype(BF16)
            zbufs[c][OWN][2 * i + 1] = jnp.concatenate([qpair[SPAN:], gpair[SPAN:]], axis=0).astype(
                BF16
            )
            return carry

        return one

    rings = {}

    def ring(c, direction, step, chunk):
        src_i = OWN if step == 1 else 2 * (step - 2) + direction
        dst_i = FAR if step == 4 else 2 * (step - 1) + direction
        part = pl.ds(chunk * CHUNK, CHUNK)
        copy = remote(
            zbufs[c][src_i].at[part], zbufs[c][dst_i].at[part],
            ring_send.at[c, direction, step - 1, chunk],
            ring_recv.at[c, direction, step - 1, chunk],
            z_peer(1 if direction == 0 else -1),
        )
        copy.start()
        rings[c, direction, step, chunk] = copy

    for chunk in range(CHUNKS):
        lax.fori_loop(2 * chunk, 2 * chunk + 2, pack(0), 0)
        for direction in range(2):
            ring(0, direction, 1, chunk)

    for chunk in range(CHUNKS):
        lax.fori_loop(2 * chunk, 2 * chunk + 2, pack(1), 0)
        for direction in range(2):
            ring(1, direction, 1, chunk)
    for tab in tabs:
        tab.wait_recv()
    to_smem = pltpu.make_async_copy(
        tabz.at[:, :, pl.ds(TAB_S, TAB_END - TAB_S)], tab_smem, local_sem.at[4]
    )
    to_smem.start()
    to_smem.wait()

    def spread(c, i):
        def one(o, carry):
            t = plane_of(o)
            sbuf[c, i, o - 1] = zbufs[c][i][tab_smem[i, 0, t]]
            remote(
                sbuf.at[c, i, o - 1], rbuf.at[c, i, t0],
                plane_send.at[c, i], plane_recv.at[c, i], plane_peer(t),
            ).start()
            return carry

        lax.fori_loop(1, PLANE, one, 0)
        rbuf[c, i, t0] = zbufs[c][i][tab_smem[i, 0, t0]]

    def pair_rows(p):
        return pl.ds(p * PAIR_ROWS, PAIR_ROWS)

    def first(c, p):
        for i in (2 * p, 2 * p + 1):
            await_bytes(rbuf.at[c, i, pl.ds(0, PLANE - 1)], plane_recv.at[c, i])

        def unpack(t, carry):
            rows = pl.ds(pl.multiple_of(p * PAIR_ROWS + t * UNIT, UNIT), UNIT)
            a = rbuf[c, 2 * p, t].astype(F32)
            b = rbuf[c, 2 * p + 1, t].astype(F32)
            qs[rows, half_cols(c)] = jnp.concatenate([a[:SPAN], b[:SPAN]], axis=0).astype(BF16)
            gs[rows, half_cols(c)] = jnp.concatenate([a[SPAN:], b[SPAN:]], axis=0).astype(BF16)
            return carry

        lax.fori_loop(0, PLANE, unpack, 0)

        def one(k, carry):
            cols = head_cols(HALF * c + k)
            scores = nt(kc[:, cols], qs[pair_rows(p), cols]) * SCALING2
            high = jnp.max(scores, axis=0, keepdims=True)
            weights = jnp.exp2(scores - high)
            total = jnp.sum(weights, axis=0, keepdims=True)
            grad_weights = nt(vc[:, cols], gs[pair_rows(p), cols])
            inner = jnp.sum(weights * grad_weights, axis=0, keepdims=True)
            stat[p, pl.ds(HALF * c + k, 1), :] = high + jnp.log(total) * LOG2E
            stat[p, pl.ds(HEADS + HALF * c + k, 1), :] = inner / total
            return carry

        lax.fori_loop(0, HALF, one, 0, unroll=HALF)

    def own_scores(cols):
        scores = nt(own_k[:, cols], own_q[:, cols]) * SCALING2
        seen = iota((ROWS, ROWS), 0) <= iota((ROWS, ROWS), 1)
        return jnp.where(seen, scores, -jnp.inf)

    def own_first(c):
        def one(k, carry):
            cols = head_cols(HALF * c + k)
            scores = own_scores(cols)
            high = jnp.max(scores, axis=0, keepdims=True)
            weights = jnp.exp2(scores - high)
            total = jnp.sum(weights, axis=0, keepdims=True)
            grad_weights = nt(own_v[:, cols], own_g[:, cols])
            inner = jnp.sum(weights * grad_weights, axis=0, keepdims=True)
            own_stat[pl.ds(HALF * c + k, 1), :] = high + jnp.log(total) * LOG2E
            own_stat[pl.ds(HEADS + HALF * c + k, 1), :] = inner / total
            return carry

        return one

    def turn_keys(h, carry):
        kt[h] = kc[:, head_cols(h)].T
        return carry

    def ring_step(c, step, work):
        for chunk in range(CHUNKS):
            for direction in range(2):
                if step == 4 and chunk // 2 != direction:
                    continue
                rings[c, direction, step, chunk].wait_recv()
                if step < 3 or (step == 3 and chunk // 2 == direction):
                    ring(c, direction, step + 1, chunk)
            work(chunk)
        if step < 4:
            spread(c, 2 * (step - 1))
            spread(c, 2 * (step - 1) + 1)
        else:
            spread(c, FAR)

    def plane_all(out, into, send, recv):
        def one(o, carry):
            t = plane_of(o)
            remote(out.at[t], into.at[t0], send, recv, plane_peer(t)).start()
            return carry

        lax.fori_loop(1, PLANE, one, 0)
        into[t0] = out[t0]

    def stats_part(p):
        return nt(pick_pair(p), stacked(stat[p]), HIGHEST)

    def stats_plane(early):
        st_out[...] = (early + stats_part(3)).reshape(PLANE, NZ, 128)
        plane_all(st_out, st_in, st_send.at[0], st_recv.at[0])

    stats_home = []

    def stats_z():
        row, lane = iota((128, 128), 0), iota((128, 128), 1)
        swap_order = ((row // PLANE == lane % NZ) & (row % PLANE == lane // NZ)).astype(F32)
        await_bytes(st_in.at[pl.ds(0, PLANE - 1)], st_recv.at[0])
        zst_out[...] = nn(swap_order, st_in[...].reshape(128, 128), HIGHEST).reshape(
            NZ, PLANE, 128
        )
        for i in range(NZ):
            j = GROUP_OF[(-OFFSETS[i]) % NZ]
            if i == OWN:
                continue
            copy = remote(
                zst_out.at[i], zst_in.at[j], zst_send.at[i], zst_recv.at[j], z_peer(OFFSETS[i])
            )
            copy.start()
            stats_home.append(copy)
        zst_in[OWN] = zst_out[OWN]

    norms_out = []

    def norms_z():
        own_slots = nt(pick_own(), stacked(own_stat[...]), HIGHEST)
        chosen = (sel_ref[...] == iota((TOPK * SPANS, 128), 1)).astype(F32)
        for copy in stats_home:
            copy.wait_recv()
        picked = nn(chosen, zst_in[...].reshape(128, 128), HIGHEST)
        logs = [own_slots] + [picked[SPANS * t:SPANS * (t + 1)] for t in range(TOPK)]
        peak = jnp.maximum(jnp.maximum(logs[0], logs[1]), jnp.maximum(logs[2], logs[3]))
        shares = [jnp.exp2(log - peak) for log in logs]
        total = (shares[0] + shares[1]) + (shares[2] + shares[3])
        norm = peak + jnp.log(total) * LOG2E
        delta = jnp.zeros((SPANS, 128), F32)
        for share, log in zip(shares, logs):
            delta += pltpu.roll(share / total, HEADS, 1) * log
        is_norm = iota((SPANS, 128), 1) % (2 * HEADS) < HEADS
        nz[OWN] = jnp.where(is_norm, norm, delta)
        for d in range(1, NZ):
            i = GROUP_OF[(-d) % NZ]
            copy = remote(nz.at[OWN], nz.at[i], nz_send.at[d], nz_recv.at[i], z_peer(d))
            copy.start()
            norms_out.append(copy)
        own_joint[...] = unstacked(tn(nz[OWN], pick_own(), HIGHEST))

    def norms_plane():
        lane8 = iota((SPANS, 128), 1) % NZ
        span_row = iota((SPANS, 128), 0)
        routes = jnp.concatenate(
            [
                jnp.where((lane8 == i) & (tabz[i, 0:1, TAB_B:TAB_S] == span_row), 1.0, 0.0)
                for i in range(NZ)
            ],
            axis=0,
        ).astype(F32)
        for copy in norms_out:
            copy.wait_recv()
        nr_out[...] = tn(routes, nz[...].reshape(128, 128), HIGHEST).reshape(PLANE, NZ, 128)
        plane_all(nr_out, nr_in, nr_send.at[0], nr_recv.at[0])

    def own_second(c):
        def one(k, carry):
            cols = head_cols(HALF * c + k)
            weights = jnp.exp2(own_scores(cols) - own_joint[pl.ds(HALF * c + k, 1), :])
            grad_weights = nt(own_v[:, cols], own_g[:, cols])
            grad_scores = weights * (grad_weights - own_joint[pl.ds(HEADS + HALF * c + k, 1), :])
            weights_low = weights.astype(BF16)
            grad_low = grad_scores.astype(BF16)
            own_gq[:, cols] = tn(grad_low, own_k[:, cols]) * SCALING
            gnk[:, cols] = (nn(grad_low, own_q[:, cols]) * SCALING).astype(BF16)
            gnv[:, cols] = nn(weights_low, own_g[:, cols]).astype(BF16)
            return carry

        lax.fori_loop(0, HALF, one, 0, unroll=2)

    def second(c, p):
        if c == 0:
            joint[p] = unstacked(tn(nr_in[...].reshape(128, 128), pick_pair(p), HIGHEST))

        def one(k, carry):
            h = HALF * c + k
            cols = head_cols(h)
            scores = nt(kc[:, cols], qs[pair_rows(p), cols]) * SCALING2
            weights = jnp.exp2(scores - joint[p, pl.ds(h, 1), :])
            grad_weights = nt(vc[:, cols], gs[pair_rows(p), cols])
            grad_scores = weights * (grad_weights - joint[p, pl.ds(HEADS + h, 1), :])
            grad_low = grad_scores.astype(BF16)
            wl[h, :, pair_rows(p)] = weights.astype(BF16)
            gl[h, :, pair_rows(p)] = grad_low
            grad_query = (nn(kt[h], grad_low) * SCALING).T
            gqb[c, p, :, :, head_cols(k)] = grad_query.reshape(PLANE, UNIT, DH).astype(BF16)
            return carry

        lax.fori_loop(0, HALF, one, 0, unroll=HALF)
        plane_all(gqb.at[c, p], gr.at[c, p], gr_send.at[c, p], gr_recv.at[c, p])

    def arrived(c, p):
        await_bytes(gr.at[c, p, pl.ds(0, PLANE - 1)], gr_recv.at[c, p])

    def span_sums(c, i, lo, n):
        p, side = i // 2, i % 2
        row, lane = iota((n, PAIR_ROWS), 0) + lo, iota((n, PAIR_ROWS), 1)
        hit = (tabz[i, 0:1, TAB_A:TAB_B] == row // SPAN) & (lane % UNIT == row % SPAN + SPAN * side)
        return nn(jnp.where(hit, 1.0, 0.0).astype(BF16), gr[c, p].reshape(PAIR_ROWS, WIDTH))

    homes = {}

    def home(c, step):
        arrived(c, 4 - step)
        for direction in range(2):
            lo, n = (direction * half, half) if step == 1 else (0, ROWS)
            rows = pl.ds(lo, n)
            i = FAR if step == 1 else 2 * (4 - step) + 1 - direction
            sums = span_sums(c, i, lo, n)
            if step == 1:
                rs_out[c, direction, 0, rows, :] = sums.astype(BF16)
            else:
                homes[c, direction, step - 1].wait_recv()
                came = pl.ds(direction * half, half) if step == 2 else rows
                rs_out[c, direction, step - 1] = sums.astype(BF16)
                if step == 2:
                    part = sums[direction * half:(direction + 1) * half]
                else:
                    part = sums
                part += rs_in[c, direction, step - 2, came, :].astype(F32)
                rs_out[c, direction, step - 1, came, :] = part.astype(BF16)
            copy = remote(
                rs_out.at[c, direction, step - 1, rows, :],
                rs_in.at[c, direction, step - 1, rows, :],
                rs_send.at[c, direction, step - 1], rs_recv.at[c, direction, step - 1],
                z_peer(1 if direction == 0 else -1),
            )
            copy.start()
            homes[c, direction, step] = copy

    def cache_grads(c):
        def one(k, carry):
            h = HALF * c + k
            cols = head_cols(h)
            gck[:, cols] = (nn(gl[h], qs[:, cols]) * SCALING).astype(BF16)
            gcv[:, cols] = nn(wl[h], gs[:, cols]).astype(BF16)
            return carry

        lax.fori_loop(0, HALF, one, 0, unroll=2)

    def finish(c):
        sums = own_gq[:, half_cols(c)] + span_sums(c, OWN, 0, ROWS)
        for direction in range(2):
            homes[c, direction, 4].wait_recv()
            sums += rs_in[c, direction, 3].astype(F32)
        gq[:, half_cols(c)] = sums.astype(BF16)

    def nothing(chunk):
        pass

    def own_work(chunk):
        lax.fori_loop(2 * (chunk % 2), 2 * (chunk % 2) + 2, own_first(chunk // 2), 0)

    def turn_work(chunk):
        lax.fori_loop(2 * chunk, 2 * chunk + 2, turn_keys, 0)

    def next_half(chunk):
        lax.fori_loop(2 * chunk, 2 * chunk + 2, pack(1), 0)
        for direction in range(2):
            ring(1, direction, 1, chunk)

    spread(0, OWN)
    spread(1, OWN)
    for i in (2, 3):
        keeps[i].wait()
        swaps[i].wait_recv()
    fetch_k.wait()
    fetch_v.wait()
    ring_step(0, 1, own_work)
    ring_step(1, 1, turn_work)
    ring_step(0, 2, nothing)
    ring_step(1, 2, nothing)
    first(0, 0)
    ring_step(0, 3, nothing)
    first(1, 0)
    ring_step(1, 3, nothing)
    first(0, 1)
    ring_step(0, 4, nothing)
    first(1, 1)
    ring_step(1, 4, nothing)
    first(0, 2)
    first(1, 2)
    first(0, 3)
    early = stats_part(0) + stats_part(1) + stats_part(2)
    first(1, 3)
    stats_plane(early)
    stats_z()
    norms_z()
    own_second(0)
    norms_plane()
    own_second(1)
    store_nk = pltpu.make_async_copy(gnk, gnk_hbm, local_sem.at[0])
    store_nv = pltpu.make_async_copy(gnv, gnv_hbm, local_sem.at[1])
    store_nk.start()
    store_nv.start()
    await_bytes(nr_in.at[pl.ds(0, PLANE - 1)], nr_recv.at[0])
    second(0, 3)
    second(1, 3)
    second(0, 2)
    second(1, 2)
    home(0, 1)
    second(0, 1)
    home(1, 1)
    second(1, 1)
    home(0, 2)
    second(0, 0)
    home(1, 2)
    second(1, 0)
    cache_grads(0)
    cache_grads(1)
    store_k = pltpu.make_async_copy(gck, gck_hbm, local_sem.at[5])
    store_v = pltpu.make_async_copy(gcv, gcv_hbm, local_sem.at[6])
    store_k.start()
    store_v.start()
    home(0, 3)
    home(1, 3)
    home(0, 4)
    home(1, 4)
    finish(0)
    finish(1)
    store_q = pltpu.make_async_copy(gq, gq_hbm, local_sem.at[2])
    store_q.start()

    for copy in swaps + tabs + stats_home + norms_out + list(rings.values()) + list(homes.values()):
        copy.wait_send()
    for c in range(NC):
        for i in range(NZ):
            await_bytes(sbuf.at[c, i], plane_send.at[c, i])
        for p in range(PAIRS):
            await_bytes(gqb.at[c, p, pl.ds(0, PLANE - 1)], gr_send.at[c, p])
    await_bytes(st_out.at[pl.ds(0, PLANE - 1)], st_send.at[0])
    await_bytes(nr_out.at[pl.ds(0, PLANE - 1)], nr_send.at[0])
    for store in (store_nk, store_nv, store_k, store_v, store_q):
        store.wait()


def hand_over(*refs):
    made, results, held, (sems,) = refs[:5], refs[5:10], refs[10:15], refs[15:]
    loads = [pltpu.make_async_copy(made[i], held[i], sems.at[0, i]) for i in range(5)]
    stores = [pltpu.make_async_copy(held[i], results[i], sems.at[1, i]) for i in range(5)]
    for load in loads:
        load.start()
    for load, store in zip(loads, stores):
        load.wait()
        store.start()
    for store in stores:
        store.wait()


def run_kernel(queries, grad_out, new_keys, new_values, cache_keys, cache_values, table, picks):
    vmem = pl.BlockSpec(memory_space=pltpu.VMEM)
    hbm = pl.BlockSpec(memory_space=pl.ANY)
    rows = jax.ShapeDtypeStruct((ROWS, FEATS), BF16)
    block = jax.ShapeDtypeStruct((BLK, FEATS), BF16)
    results = (rows, rows, rows, block, block)
    dma = pltpu.SemaphoreType.DMA
    units = (PLANE, UNIT, WIDTH)
    made = pl.pallas_call(
        kernel,
        out_shape=results,
        in_specs=[hbm] * 6 + [vmem] * 2,
        out_specs=(hbm,) * 5,
        scratch_shapes=[
            *[pltpu.VMEM((ROWS, FEATS), BF16)] * 4,
            *[pltpu.VMEM((BLK, FEATS), BF16)] * 2,
            pltpu.VMEM((HEADS, DH, BLK), BF16),
            [[pltpu.VMEM((SPANS + 1, UNIT, WIDTH), BF16)] * NZ] * NC,
            pltpu.VMEM((NC, NZ, PLANE - 1, UNIT, WIDTH), BF16),
            pltpu.VMEM((NC, NZ) + units, BF16),
            *[pltpu.VMEM((NZ, SPAN, TAB_END), jnp.int32)] * 2,
            pltpu.SMEM((NZ, SPAN, TAB_END - TAB_S), jnp.int32),
            *[pltpu.VMEM((PAIRS * PAIR_ROWS, FEATS), BF16)] * 2,
            *[pltpu.VMEM((HEADS, BLK, PAIRS * PAIR_ROWS), BF16)] * 2,
            pltpu.VMEM((PAIRS, 2 * HEADS, PAIR_ROWS), F32),
            pltpu.VMEM((2 * HEADS, ROWS), F32),
            *[pltpu.VMEM((PLANE, NZ, 128), F32)] * 2,
            *[pltpu.VMEM((NZ, PLANE, 128), F32)] * 2,
            pltpu.VMEM((NZ, SPANS, 128), F32),
            *[pltpu.VMEM((PLANE, NZ, 128), F32)] * 2,
            pltpu.VMEM((PAIRS, 2 * HEADS, PAIR_ROWS), F32),
            pltpu.VMEM((2 * HEADS, ROWS), F32),
            *[pltpu.VMEM((NC, PAIRS) + units, BF16)] * 2,
            *[pltpu.VMEM((NC, 2, 4, ROWS, WIDTH), BF16)] * 2,
            pltpu.VMEM((ROWS, FEATS), F32),
            *[pltpu.VMEM((ROWS, FEATS), BF16)] * 3,
            *[pltpu.VMEM((BLK, FEATS), BF16)] * 2,
            dma((4,)), dma((4,)), dma((7,)),
            dma((NZ,)), dma((NZ,)),
            dma((NC, 2, 4, CHUNKS)), dma((NC, 2, 4, CHUNKS)),
            dma((NC, NZ)), dma((NC, NZ)),
            dma((1,)), dma((1,)), dma((NZ,)), dma((NZ,)),
            dma((NZ,)), dma((NZ,)), dma((1,)), dma((1,)),
            dma((NC, PAIRS)), dma((NC, PAIRS)),
            dma((NC, 2, 4)), dma((NC, 2, 4)),
        ],
        compiler_params=pltpu.CompilerParams(
            collective_id=0, has_side_effects=True, vmem_limit_bytes=60 * 1024 * 1024
        ),
    )(queries, grad_out, new_keys, new_values, cache_keys, cache_values, table, picks)
    return pl.pallas_call(
        hand_over,
        out_shape=results,
        in_specs=[hbm] * 5,
        out_specs=(hbm,) * 5,
        scratch_shapes=[*[pltpu.VMEM(x.shape, BF16) for x in results], dma((2, 5))],
        compiler_params=pltpu.CompilerParams(vmem_limit_bytes=60 * 1024 * 1024),
    )(*made)


def body(queries, new_keys, new_values, grad_out, cache_keys, cache_values, choices):
    z = lax.axis_index("seq") // PLANE
    lanes = jnp.concatenate(
        [
            jnp.arange(256, dtype=jnp.int32) // UNIT,
            jnp.arange(128, dtype=jnp.int32) // NZ,
            jnp.arange(128, dtype=jnp.int32) % PLANE,
        ]
    )
    blocks = jnp.arange(NZ, dtype=jnp.int32)[:, None] * PLANE + lanes[None, :]
    hits = choices[:, :, None, None] == blocks[None, None]
    spans = jnp.arange(SPANS, dtype=jnp.int32)[:, None, None, None]
    table = jnp.min(jnp.where(hits, spans, SPANS), axis=(0, 1))
    away = (choices // PLANE - z) % NZ
    group = jnp.where(away == 0, OWN, jnp.where(away < 4, 2 * away - 1, 14 - 2 * away))
    group = jnp.where(away == 4, FAR, group)
    picks = (group * PLANE + choices % PLANE).T.reshape(TOPK * SPANS, 1)
    return run_kernel(
        queries, grad_out, new_keys, new_values, cache_keys, cache_values, table, picks
    )


def solution(mesh):
    rows = P(("seq", "head"), None)
    both = P("seq", "head")
    return jax.shard_map(
        body,
        mesh=mesh,
        in_specs=(rows, rows, rows, rows, both, both, P("seq", None)),
        out_specs=(both,) * 5,
        check_vma=False,
    )
```

```python
import math

import jax
import jax.numpy as jnp
from jax import lax
from jax.experimental import pallas as pl
from jax.experimental.pallas import tpu as pltpu
from jax.sharding import PartitionSpec as P

DH = 128
SPAN = 8
TOPK = 3
NZ = 8
NX = 4
NY = 4
PLANE = NX * NY
SPANS = 16
FEATS = 1024
HEADS = FEATS // DH
ROWS = SPANS * SPAN
BLK = 512
PAIRS = NZ // 2
PAIR_ROWS = 2 * PLANE * SPAN
UNIT = 2 * SPAN
CHUNKS = 4
NC = 2
WIDTH = FEATS // NC
HALF = HEADS // NC
CHUNK = SPANS // CHUNKS
SCALING = 1.0 / math.sqrt(DH)
LOG2E = math.log2(math.e)
SCALING2 = SCALING * LOG2E
MESH = pl.DeviceIdType.MESH
OFFSETS = (-1, 1, -2, 2, -3, 3, 0, 4)
GROUP_OF = (6, 1, 3, 5, 7, 4, 2, 0)
OWN = 6
FAR = 7
TAB_A, TAB_B, TAB_S, TAB_END = 0, 256, 384, 512
BF16 = jnp.bfloat16
F32 = jnp.float32
HIGHEST = lax.Precision.HIGHEST


def iota(shape, axis):
    return lax.broadcasted_iota(jnp.int32, shape, axis)


def nt(a, b, precision=None):
    return lax.dot_general(
        a, b, (((1,), (1,)), ((), ())), precision=precision, preferred_element_type=F32
    )


def tn(a, b, precision=None):
    return lax.dot_general(
        a, b, (((0,), (0,)), ((), ())), precision=precision, preferred_element_type=F32
    )


def nn(a, b, precision=None):
    return jnp.dot(a, b, precision=precision, preferred_element_type=F32)


def lane_mask(lanes):
    return iota((128, lanes), 0) // 16 == iota((128, lanes), 1) % SPAN


def pick_pair(p):
    row, lane = iota((128, PAIR_ROWS), 0), iota((128, PAIR_ROWS), 1)
    hit = (row // NZ == lane // UNIT) & (row % NZ == 2 * p + (lane // SPAN) % 2)
    return hit.astype(F32)


def pick_own():
    return (iota((SPANS, ROWS), 0) == iota((SPANS, ROWS), 1) // SPAN).astype(F32)


def stacked(stats):
    tall = jnp.concatenate([stats] * SPAN, axis=0)
    return jnp.where(lane_mask(stats.shape[1]), tall, 0.0)


def unstacked(wide):
    kept = jnp.where(lane_mask(wide.shape[1]), wide, 0.0)
    return jnp.sum(kept.reshape(SPAN, 2 * HEADS, wide.shape[1]), axis=0)


def head_cols(h):
    return pl.ds(pl.multiple_of(h * DH, DH), DH)


def kernel(
    q_hbm, g_hbm, k_hbm, v_hbm, ck_hbm, cv_hbm, tab_ref, sel_ref,
    gq_hbm, gnk_hbm, gnv_hbm, gck_hbm, gcv_hbm,
    own_q, own_g, own_k, own_v, kc, vc, kt,
    zbufs, sbuf, rbuf, tab_src, tabz, tab_smem, qs, gs, wl, gl,
    stat, own_stat, st_out, st_in, zst_out, zst_in, nz, nr_out, nr_in, joint, own_joint,
    gqb, gr, rs_out, rs_in, own_gq, gq, gnk, gnv, gck, gcv,
    head_send, head_recv, local_sem, tab_send, tab_recv, ring_send, ring_recv,
    plane_send, plane_recv, st_send, st_recv, zst_send, zst_recv, nz_send, nz_recv,
    nr_send, nr_recv, gr_send, gr_recv, rs_send, rs_recv,
):
    seq = lax.axis_index("seq")
    head = lax.axis_index("head")
    z = seq // PLANE
    t0 = seq % PLANE
    x0 = t0 // NY
    y0 = t0 % NY

    def z_peer(d):
        return (((z + d) % NZ) * PLANE + t0, head)

    def plane_of(o):
        m = (5 * o) % PLANE
        return ((x0 + m // NY) % NX) * NY + (y0 + m % NY) % NY

    def plane_peer(t):
        return (z * PLANE + t, head)

    def remote(src, dst, send, recv, device):
        return pltpu.make_async_remote_copy(
            src_ref=src, dst_ref=dst, send_sem=send, recv_sem=recv,
            device_id=device, device_id_type=MESH,
        )

    def await_bytes(ref, sem):
        pltpu.make_async_copy(ref, ref, sem).wait()

    half = ROWS // 2
    my_rows = pl.ds(pl.multiple_of(head * half, half), half)
    my_cols = pl.ds(pl.multiple_of(head * FEATS, FEATS), FEATS)
    other_cols = pl.ds(pl.multiple_of((1 - head) * FEATS, FEATS), FEATS)
    sources = ((q_hbm, own_q), (g_hbm, own_g), (k_hbm, own_k), (v_hbm, own_v))
    keeps = [
        pltpu.make_async_copy(src.at[:, my_cols], dst.at[my_rows, :], local_sem.at[i])
        for i, (src, dst) in enumerate(sources)
    ]
    for keep in keeps:
        keep.start()
    fetch_k = pltpu.make_async_copy(ck_hbm, kc, local_sem.at[5])
    fetch_v = pltpu.make_async_copy(cv_hbm, vc, local_sem.at[6])
    fetch_k.start()
    fetch_v.start()

    sibling = (seq, 1 - head)
    barrier = pltpu.get_barrier_semaphore()
    pl.semaphore_signal(barrier, inc=1, device_id=sibling, device_id_type=MESH)
    for d in range(1, NZ):
        pl.semaphore_signal(barrier, inc=1, device_id=z_peer(d), device_id_type=MESH)

    def greet(o, carry):
        pl.semaphore_signal(
            barrier, inc=1, device_id=plane_peer(plane_of(o)), device_id_type=MESH
        )
        return carry

    lax.fori_loop(1, PLANE, greet, 0, unroll=PLANE - 1)
    for c in range(NC):
        for i in range(NZ):
            zbufs[c][i][SPANS] = jnp.zeros((UNIT, WIDTH), BF16)
    for plane in range(NZ):
        tab_src[plane] = jnp.broadcast_to(tab_ref[plane:plane + 1, :], (SPAN, TAB_END))
    tabz[OWN] = tab_src[z]
    pl.semaphore_wait(barrier, 1 + (NZ - 1) + (PLANE - 1))

    swaps = [
        remote(src.at[:, other_cols], dst.at[my_rows, :], head_send.at[i], head_recv.at[i], sibling)
        for i, (src, dst) in enumerate(sources)
    ]
    for swap in swaps[:2]:
        swap.start()
    tabs = []
    for d in range(1, NZ):
        i = GROUP_OF[(-d) % NZ]
        tab = remote(tab_src.at[(z + d) % NZ], tabz.at[i], tab_send.at[d], tab_recv.at[i], z_peer(d))
        tab.start()
        tabs.append(tab)
    for swap in swaps[2:]:
        swap.start()
    for i in (0, 1):
        keeps[i].wait()
        swaps[i].wait_recv()

    def half_cols(c):
        return pl.ds(c * WIDTH, WIDTH)

    def pack(c):
        def one(i, carry):
            rows = pl.ds(pl.multiple_of(UNIT * i, UNIT), UNIT)
            qpair = own_q[rows, half_cols(c)].astype(F32)
            gpair = own_g[rows, half_cols(c)].astype(F32)
            zbufs[c][OWN][2 * i] = jnp.concatenate([qpair[:SPAN], gpair[:SPAN]], axis=0).astype(BF16)
            zbufs[c][OWN][2 * i + 1] = jnp.concatenate([qpair[SPAN:], gpair[SPAN:]], axis=0).astype(
                BF16
            )
            return carry

        return one

    rings = {}

    def ring(c, direction, step, chunk):
        src_i = OWN if step == 1 else 2 * (step - 2) + direction
        dst_i = FAR if step == 4 else 2 * (step - 1) + direction
        part = pl.ds(chunk * CHUNK, CHUNK)
        copy = remote(
            zbufs[c][src_i].at[part], zbufs[c][dst_i].at[part],
            ring_send.at[c, direction, step - 1, chunk],
            ring_recv.at[c, direction, step - 1, chunk],
            z_peer(1 if direction == 0 else -1),
        )
        copy.start()
        rings[c, direction, step, chunk] = copy

    for chunk in range(CHUNKS):
        lax.fori_loop(2 * chunk, 2 * chunk + 2, pack(0), 0)
        for direction in range(2):
            ring(0, direction, 1, chunk)

    for chunk in range(CHUNKS):
        lax.fori_loop(2 * chunk, 2 * chunk + 2, pack(1), 0)
        for direction in range(2):
            ring(1, direction, 1, chunk)
    for tab in tabs:
        tab.wait_recv()
    to_smem = pltpu.make_async_copy(
        tabz.at[:, :, pl.ds(TAB_S, TAB_END - TAB_S)], tab_smem, local_sem.at[4]
    )
    to_smem.start()
    to_smem.wait()

    def spread(c, i):
        def one(o, carry):
            t = plane_of(o)
            sbuf[c, i, o - 1] = zbufs[c][i][tab_smem[i, 0, t]]
            remote(
                sbuf.at[c, i, o - 1], rbuf.at[c, i, t0],
                plane_send.at[c, i], plane_recv.at[c, i], plane_peer(t),
            ).start()
            return carry

        lax.fori_loop(1, PLANE, one, 0, unroll=PLANE - 1)
        rbuf[c, i, t0] = zbufs[c][i][tab_smem[i, 0, t0]]

    def pair_rows(p):
        return pl.ds(p * PAIR_ROWS, PAIR_ROWS)

    def first(c, p):
        for i in (2 * p, 2 * p + 1):
            await_bytes(rbuf.at[c, i, pl.ds(0, PLANE - 1)], plane_recv.at[c, i])

        def unpack(t, carry):
            rows = pl.ds(pl.multiple_of(p * PAIR_ROWS + t * UNIT, UNIT), UNIT)
            a = rbuf[c, 2 * p, t].astype(F32)
            b = rbuf[c, 2 * p + 1, t].astype(F32)
            qs[rows, half_cols(c)] = jnp.concatenate([a[:SPAN], b[:SPAN]], axis=0).astype(BF16)
            gs[rows, half_cols(c)] = jnp.concatenate([a[SPAN:], b[SPAN:]], axis=0).astype(BF16)
            return carry

        lax.fori_loop(0, PLANE, unpack, 0, unroll=4)

        def one(k, carry):
            cols = head_cols(HALF * c + k)
            scores = nt(kc[:, cols], qs[pair_rows(p), cols]) * SCALING2
            high = jnp.max(scores, axis=0, keepdims=True)
            weights = jnp.exp2(scores - high)
            total = jnp.sum(weights, axis=0, keepdims=True)
            grad_weights = nt(vc[:, cols], gs[pair_rows(p), cols])
            inner = jnp.sum(weights * grad_weights, axis=0, keepdims=True)
            stat[p, pl.ds(HALF * c + k, 1), :] = high + jnp.log(total) * LOG2E
            stat[p, pl.ds(HEADS + HALF * c + k, 1), :] = inner / total
            return carry

        lax.fori_loop(0, HALF, one, 0, unroll=HALF)

    def own_scores(cols):
        scores = nt(own_k[:, cols], own_q[:, cols]) * SCALING2
        seen = iota((ROWS, ROWS), 0) <= iota((ROWS, ROWS), 1)
        return jnp.where(seen, scores, -jnp.inf)

    def own_first(c):
        def one(k, carry):
            cols = head_cols(HALF * c + k)
            scores = own_scores(cols)
            high = jnp.max(scores, axis=0, keepdims=True)
            weights = jnp.exp2(scores - high)
            total = jnp.sum(weights, axis=0, keepdims=True)
            grad_weights = nt(own_v[:, cols], own_g[:, cols])
            inner = jnp.sum(weights * grad_weights, axis=0, keepdims=True)
            own_stat[pl.ds(HALF * c + k, 1), :] = high + jnp.log(total) * LOG2E
            own_stat[pl.ds(HEADS + HALF * c + k, 1), :] = inner / total
            return carry

        return one

    def turn_keys(h, carry):
        kt[h] = kc[:, head_cols(h)].T
        return carry

    def ring_step(c, step, work):
        for chunk in range(CHUNKS):
            for direction in range(2):
                if step == 4 and chunk // 2 != direction:
                    continue
                rings[c, direction, step, chunk].wait_recv()
                if step < 3 or (step == 3 and chunk // 2 == direction):
                    ring(c, direction, step + 1, chunk)
            work(chunk)
        if step < 4:
            spread(c, 2 * (step - 1))
            spread(c, 2 * (step - 1) + 1)
        else:
            spread(c, FAR)

    def plane_all(out, into, send, recv):
        def one(o, carry):
            t = plane_of(o)
            remote(out.at[t], into.at[t0], send, recv, plane_peer(t)).start()
            return carry

        lax.fori_loop(1, PLANE, one, 0, unroll=PLANE - 1)
        into[t0] = out[t0]

    def stats_part(p):
        return nt(pick_pair(p), stacked(stat[p]), HIGHEST)

    def stats_plane(early):
        st_out[...] = (early + stats_part(3)).reshape(PLANE, NZ, 128)
        plane_all(st_out, st_in, st_send.at[0], st_recv.at[0])

    stats_home = []

    def stats_z():
        row, lane = iota((128, 128), 0), iota((128, 128), 1)
        swap_order = ((row // PLANE == lane % NZ) & (row % PLANE == lane // NZ)).astype(F32)
        await_bytes(st_in.at[pl.ds(0, PLANE - 1)], st_recv.at[0])
        zst_out[...] = nn(swap_order, st_in[...].reshape(128, 128), HIGHEST).reshape(
            NZ, PLANE, 128
        )
        for i in range(NZ):
            j = GROUP_OF[(-OFFSETS[i]) % NZ]
            if i == OWN:
                continue
            copy = remote(
                zst_out.at[i], zst_in.at[j], zst_send.at[i], zst_recv.at[j], z_peer(OFFSETS[i])
            )
            copy.start()
            stats_home.append(copy)
        zst_in[OWN] = zst_out[OWN]

    norms_out = []

    def norms_z():
        own_slots = nt(pick_own(), stacked(own_stat[...]), HIGHEST)
        chosen = (sel_ref[...] == iota((TOPK * SPANS, 128), 1)).astype(F32)
        for copy in stats_home:
            copy.wait_recv()
        picked = nn(chosen, zst_in[...].reshape(128, 128), HIGHEST)
        logs = [own_slots] + [picked[SPANS * t:SPANS * (t + 1)] for t in range(TOPK)]
        peak = jnp.maximum(jnp.maximum(logs[0], logs[1]), jnp.maximum(logs[2], logs[3]))
        shares = [jnp.exp2(log - peak) for log in logs]
        total = (shares[0] + shares[1]) + (shares[2] + shares[3])
        norm = peak + jnp.log(total) * LOG2E
        delta = jnp.zeros((SPANS, 128), F32)
        for share, log in zip(shares, logs):
            delta += pltpu.roll(share / total, HEADS, 1) * log
        is_norm = iota((SPANS, 128), 1) % (2 * HEADS) < HEADS
        nz[OWN] = jnp.where(is_norm, norm, delta)
        for d in range(1, NZ):
            i = GROUP_OF[(-d) % NZ]
            copy = remote(nz.at[OWN], nz.at[i], nz_send.at[d], nz_recv.at[i], z_peer(d))
            copy.start()
            norms_out.append(copy)
        own_joint[...] = unstacked(tn(nz[OWN], pick_own(), HIGHEST))

    def norms_plane():
        lane8 = iota((SPANS, 128), 1) % NZ
        span_row = iota((SPANS, 128), 0)
        routes = jnp.concatenate(
            [
                jnp.where((lane8 == i) & (tabz[i, 0:1, TAB_B:TAB_S] == span_row), 1.0, 0.0)
                for i in range(NZ)
            ],
            axis=0,
        ).astype(F32)
        for copy in norms_out:
            copy.wait_recv()
        nr_out[...] = tn(routes, nz[...].reshape(128, 128), HIGHEST).reshape(PLANE, NZ, 128)
        plane_all(nr_out, nr_in, nr_send.at[0], nr_recv.at[0])

    def own_second(c):
        def one(k, carry):
            cols = head_cols(HALF * c + k)
            weights = jnp.exp2(own_scores(cols) - own_joint[pl.ds(HALF * c + k, 1), :])
            grad_weights = nt(own_v[:, cols], own_g[:, cols])
            grad_scores = weights * (grad_weights - own_joint[pl.ds(HEADS + HALF * c + k, 1), :])
            weights_low = weights.astype(BF16)
            grad_low = grad_scores.astype(BF16)
            own_gq[:, cols] = tn(grad_low, own_k[:, cols]) * SCALING
            gnk[:, cols] = (nn(grad_low, own_q[:, cols]) * SCALING).astype(BF16)
            gnv[:, cols] = nn(weights_low, own_g[:, cols]).astype(BF16)
            return carry

        lax.fori_loop(0, HALF, one, 0, unroll=2)

    def second(c, p):
        if c == 0:
            joint[p] = unstacked(tn(nr_in[...].reshape(128, 128), pick_pair(p), HIGHEST))

        def one(k, carry):
            h = HALF * c + k
            cols = head_cols(h)
            scores = nt(kc[:, cols], qs[pair_rows(p), cols]) * SCALING2
            weights = jnp.exp2(scores - joint[p, pl.ds(h, 1), :])
            grad_weights = nt(vc[:, cols], gs[pair_rows(p), cols])
            grad_scores = weights * (grad_weights - joint[p, pl.ds(HEADS + h, 1), :])
            grad_low = grad_scores.astype(BF16)
            wl[h, :, pair_rows(p)] = weights.astype(BF16)
            gl[h, :, pair_rows(p)] = grad_low
            grad_query = (nn(kt[h], grad_low) * SCALING).T
            gqb[c, p, :, :, head_cols(k)] = grad_query.reshape(PLANE, UNIT, DH).astype(BF16)
            return carry

        lax.fori_loop(0, HALF, one, 0, unroll=HALF)
        plane_all(gqb.at[c, p], gr.at[c, p], gr_send.at[c, p], gr_recv.at[c, p])

    def arrived(c, p):
        await_bytes(gr.at[c, p, pl.ds(0, PLANE - 1)], gr_recv.at[c, p])

    def span_sums(c, i, lo, n):
        p, side = i // 2, i % 2
        row, lane = iota((n, PAIR_ROWS), 0) + lo, iota((n, PAIR_ROWS), 1)
        hit = (tabz[i, 0:1, TAB_A:TAB_B] == row // SPAN) & (lane % UNIT == row % SPAN + SPAN * side)
        return nn(jnp.where(hit, 1.0, 0.0).astype(BF16), gr[c, p].reshape(PAIR_ROWS, WIDTH))

    homes = {}

    def home(c, step):
        arrived(c, 4 - step)
        for direction in range(2):
            lo, n = (direction * half, half) if step == 1 else (0, ROWS)
            rows = pl.ds(lo, n)
            i = FAR if step == 1 else 2 * (4 - step) + 1 - direction
            sums = span_sums(c, i, lo, n)
            if step == 1:
                rs_out[c, direction, 0, rows, :] = sums.astype(BF16)
            else:
                homes[c, direction, step - 1].wait_recv()
                came = pl.ds(direction * half, half) if step == 2 else rows
                rs_out[c, direction, step - 1] = sums.astype(BF16)
                if step == 2:
                    part = sums[direction * half:(direction + 1) * half]
                else:
                    part = sums
                part += rs_in[c, direction, step - 2, came, :].astype(F32)
                rs_out[c, direction, step - 1, came, :] = part.astype(BF16)
            copy = remote(
                rs_out.at[c, direction, step - 1, rows, :],
                rs_in.at[c, direction, step - 1, rows, :],
                rs_send.at[c, direction, step - 1], rs_recv.at[c, direction, step - 1],
                z_peer(1 if direction == 0 else -1),
            )
            copy.start()
            homes[c, direction, step] = copy

    def cache_grads(c):
        def one(k, carry):
            h = HALF * c + k
            cols = head_cols(h)
            gck[:, cols] = (nn(gl[h], qs[:, cols]) * SCALING).astype(BF16)
            gcv[:, cols] = nn(wl[h], gs[:, cols]).astype(BF16)
            return carry

        lax.fori_loop(0, HALF, one, 0, unroll=2)

    def finish(c):
        sums = own_gq[:, half_cols(c)] + span_sums(c, OWN, 0, ROWS)
        for direction in range(2):
            homes[c, direction, 4].wait_recv()
            sums += rs_in[c, direction, 3].astype(F32)
        gq[:, half_cols(c)] = sums.astype(BF16)

    def nothing(chunk):
        pass

    def own_work(chunk):
        lax.fori_loop(2 * (chunk % 2), 2 * (chunk % 2) + 2, own_first(chunk // 2), 0)

    def turn_work(chunk):
        lax.fori_loop(2 * chunk, 2 * chunk + 2, turn_keys, 0)

    def next_half(chunk):
        lax.fori_loop(2 * chunk, 2 * chunk + 2, pack(1), 0)
        for direction in range(2):
            ring(1, direction, 1, chunk)

    spread(0, OWN)
    spread(1, OWN)
    for i in (2, 3):
        keeps[i].wait()
        swaps[i].wait_recv()
    fetch_k.wait()
    fetch_v.wait()
    ring_step(0, 1, own_work)
    ring_step(1, 1, turn_work)
    ring_step(0, 2, nothing)
    ring_step(1, 2, nothing)
    first(0, 0)
    ring_step(0, 3, nothing)
    first(1, 0)
    ring_step(1, 3, nothing)
    first(0, 1)
    ring_step(0, 4, nothing)
    first(1, 1)
    ring_step(1, 4, nothing)
    first(0, 2)
    first(1, 2)
    first(0, 3)
    early = stats_part(0) + stats_part(1) + stats_part(2)
    first(1, 3)
    stats_plane(early)
    stats_z()
    norms_z()
    own_second(0)
    norms_plane()
    own_second(1)
    store_nk = pltpu.make_async_copy(gnk, gnk_hbm, local_sem.at[0])
    store_nv = pltpu.make_async_copy(gnv, gnv_hbm, local_sem.at[1])
    store_nk.start()
    store_nv.start()
    await_bytes(nr_in.at[pl.ds(0, PLANE - 1)], nr_recv.at[0])
    second(0, 3)
    second(1, 3)
    second(0, 2)
    second(1, 2)
    home(0, 1)
    second(0, 1)
    home(1, 1)
    second(1, 1)
    home(0, 2)
    second(0, 0)
    home(1, 2)
    second(1, 0)
    cache_grads(0)
    cache_grads(1)
    store_k = pltpu.make_async_copy(gck, gck_hbm, local_sem.at[5])
    store_v = pltpu.make_async_copy(gcv, gcv_hbm, local_sem.at[6])
    store_k.start()
    store_v.start()
    home(0, 3)
    home(1, 3)
    home(0, 4)
    home(1, 4)
    finish(0)
    finish(1)
    store_q = pltpu.make_async_copy(gq, gq_hbm, local_sem.at[2])
    store_q.start()

    for copy in swaps + tabs + stats_home + norms_out + list(rings.values()) + list(homes.values()):
        copy.wait_send()
    for c in range(NC):
        for i in range(NZ):
            await_bytes(sbuf.at[c, i], plane_send.at[c, i])
        for p in range(PAIRS):
            await_bytes(gqb.at[c, p, pl.ds(0, PLANE - 1)], gr_send.at[c, p])
    await_bytes(st_out.at[pl.ds(0, PLANE - 1)], st_send.at[0])
    await_bytes(nr_out.at[pl.ds(0, PLANE - 1)], nr_send.at[0])
    for store in (store_nk, store_nv, store_k, store_v, store_q):
        store.wait()


def hand_over(*refs):
    made, results, held, (sems,) = refs[:5], refs[5:10], refs[10:15], refs[15:]
    loads = [pltpu.make_async_copy(made[i], held[i], sems.at[0, i]) for i in range(5)]
    stores = [pltpu.make_async_copy(held[i], results[i], sems.at[1, i]) for i in range(5)]
    for load in loads:
        load.start()
    for load, store in zip(loads, stores):
        load.wait()
        store.start()
    for store in stores:
        store.wait()


def run_kernel(queries, grad_out, new_keys, new_values, cache_keys, cache_values, table, picks):
    vmem = pl.BlockSpec(memory_space=pltpu.VMEM)
    hbm = pl.BlockSpec(memory_space=pl.ANY)
    rows = jax.ShapeDtypeStruct((ROWS, FEATS), BF16)
    block = jax.ShapeDtypeStruct((BLK, FEATS), BF16)
    results = (rows, rows, rows, block, block)
    dma = pltpu.SemaphoreType.DMA
    units = (PLANE, UNIT, WIDTH)
    made = pl.pallas_call(
        kernel,
        out_shape=results,
        in_specs=[hbm] * 6 + [vmem] * 2,
        out_specs=(hbm,) * 5,
        scratch_shapes=[
            *[pltpu.VMEM((ROWS, FEATS), BF16)] * 4,
            *[pltpu.VMEM((BLK, FEATS), BF16)] * 2,
            pltpu.VMEM((HEADS, DH, BLK), BF16),
            [[pltpu.VMEM((SPANS + 1, UNIT, WIDTH), BF16)] * NZ] * NC,
            pltpu.VMEM((NC, NZ, PLANE - 1, UNIT, WIDTH), BF16),
            pltpu.VMEM((NC, NZ) + units, BF16),
            *[pltpu.VMEM((NZ, SPAN, TAB_END), jnp.int32)] * 2,
            pltpu.SMEM((NZ, SPAN, TAB_END - TAB_S), jnp.int32),
            *[pltpu.VMEM((PAIRS * PAIR_ROWS, FEATS), BF16)] * 2,
            *[pltpu.VMEM((HEADS, BLK, PAIRS * PAIR_ROWS), BF16)] * 2,
            pltpu.VMEM((PAIRS, 2 * HEADS, PAIR_ROWS), F32),
            pltpu.VMEM((2 * HEADS, ROWS), F32),
            *[pltpu.VMEM((PLANE, NZ, 128), F32)] * 2,
            *[pltpu.VMEM((NZ, PLANE, 128), F32)] * 2,
            pltpu.VMEM((NZ, SPANS, 128), F32),
            *[pltpu.VMEM((PLANE, NZ, 128), F32)] * 2,
            pltpu.VMEM((PAIRS, 2 * HEADS, PAIR_ROWS), F32),
            pltpu.VMEM((2 * HEADS, ROWS), F32),
            *[pltpu.VMEM((NC, PAIRS) + units, BF16)] * 2,
            *[pltpu.VMEM((NC, 2, 4, ROWS, WIDTH), BF16)] * 2,
            pltpu.VMEM((ROWS, FEATS), F32),
            *[pltpu.VMEM((ROWS, FEATS), BF16)] * 3,
            *[pltpu.VMEM((BLK, FEATS), BF16)] * 2,
            dma((4,)), dma((4,)), dma((7,)),
            dma((NZ,)), dma((NZ,)),
            dma((NC, 2, 4, CHUNKS)), dma((NC, 2, 4, CHUNKS)),
            dma((NC, NZ)), dma((NC, NZ)),
            dma((1,)), dma((1,)), dma((NZ,)), dma((NZ,)),
            dma((NZ,)), dma((NZ,)), dma((1,)), dma((1,)),
            dma((NC, PAIRS)), dma((NC, PAIRS)),
            dma((NC, 2, 4)), dma((NC, 2, 4)),
        ],
        compiler_params=pltpu.CompilerParams(
            collective_id=0, has_side_effects=True, vmem_limit_bytes=60 * 1024 * 1024
        ),
    )(queries, grad_out, new_keys, new_values, cache_keys, cache_values, table, picks)
    return pl.pallas_call(
        hand_over,
        out_shape=results,
        in_specs=[hbm] * 5,
        out_specs=(hbm,) * 5,
        scratch_shapes=[*[pltpu.VMEM(x.shape, BF16) for x in results], dma((2, 5))],
        compiler_params=pltpu.CompilerParams(vmem_limit_bytes=60 * 1024 * 1024),
    )(*made)


def body(queries, new_keys, new_values, grad_out, cache_keys, cache_values, choices):
    z = lax.axis_index("seq") // PLANE
    lanes = jnp.concatenate(
        [
            jnp.arange(256, dtype=jnp.int32) // UNIT,
            jnp.arange(128, dtype=jnp.int32) // NZ,
            jnp.arange(128, dtype=jnp.int32) % PLANE,
        ]
    )
    blocks = jnp.arange(NZ, dtype=jnp.int32)[:, None] * PLANE + lanes[None, :]
    hits = choices[:, :, None, None] == blocks[None, None]
    spans = jnp.arange(SPANS, dtype=jnp.int32)[:, None, None, None]
    table = jnp.min(jnp.where(hits, spans, SPANS), axis=(0, 1))
    away = (choices // PLANE - z) % NZ
    group = jnp.where(away == 0, OWN, jnp.where(away < 4, 2 * away - 1, 14 - 2 * away))
    group = jnp.where(away == 4, FAR, group)
    picks = (group * PLANE + choices % PLANE).T.reshape(TOPK * SPANS, 1)
    return run_kernel(
        queries, grad_out, new_keys, new_values, cache_keys, cache_values, table, picks
    )


def solution(mesh):
    rows = P(("seq", "head"), None)
    both = P("seq", "head")
    return jax.shard_map(
        body,
        mesh=mesh,
        in_specs=(rows, rows, rows, rows, both, both, P("seq", None)),
        out_specs=(both,) * 5,
        check_vma=False,
    )
```
